32 devices in a mesh: groups: 2 (over y), cent: 4 (over z), rows: 2 (over x), sub: 2 (over core).
Axes of the slice: x: 2, y: 2, z: 4, core: 2. Of those that a mesh axis runs over, the one named last changes fastest.
Arguments:
- embeddings: bfloat16 [4096, 768], P(('groups', 'cent', 'rows', 'sub')), parts along dimension 0, may hold values from -6 to 6
- coarse_lists: int32 [4096, 8], P(('groups', 'cent', 'rows', 'sub')), parts along dimension 0, may hold values from 0 to 127, all different within a row; in each aligned block of 128 rows (0 to 127, 128 to 255, ...) at most 16 rows name the same one
- coarse_table: bfloat16 [128, 768], replicated, may hold values from -6 to 6
- fine_table: bfloat16 [8192, 768], P(('cent', 'rows', 'sub')), may hold values from -6 to 6
Outputs:
- fine_out: bfloat16 [16384, 768], P(('groups', 'cent', 'rows', 'sub')), parts along dimension 0
- row_cost: float32 [4096], P(('groups', 'cent', 'rows', 'sub')), parts along dimension 0
- log_weights: float32 [256], P(('groups', 'cent', 'rows', 'sub')), parts along dimension 0
The draws below stay inside these ranges and needn't reach their ends.
There are 2 independent parts, one for each index of `groups`. The reference program is written for one: setup_inputs(seed, part) draws one part's arguments, and reference() takes and returns one part's arrays. A program takes and returns all parts, laid end to end along the dimension named above; an argument that names none is the same for every part. Nothing has to cross between parts.
Inputs may be any that keep to these rules, and one draw needn't show every extreme that they name: `coarse_lists`: each row lists 8 different coarse clusters; among the rows of one device no cluster is listed by more than 16 rows, and in every draw some cluster is listed by exactly 16 rows of some device.
All inputs are finite; a program needn't handle non-finite values.
Results may differ from the reference program's by a relative error of at most 0.0024.
Values may be sent and summed in bfloat16 or wider, within the bound.
A program may use at most 64 MiB of HBM per device.

```python
import math
import jax
import jax.numpy as jnp
import numpy as np
from jax import lax

D = 768
FINE_PER = 64
TOP = 8
ITERS = 2
ROW_DEV = 128
ROWS = 2048
COARSE = 128
FINE = 8192
MOST = 16


def levels(stream_key, shape, cuts, least, high):
    loudness, own = 1.0, jax.random.fold_in(stream_key, 6)
    for dim, shards_of in cuts:
        draws = jnp.exp(jax.random.uniform(jax.random.fold_in(own, dim), (shards_of,), jnp.float32, least / len(cuts), high / len(cuts)))
        loudness = loudness * jnp.repeat(draws, shape[dim] // shards_of).reshape([-1 if axis == dim else 1 for axis in range(len(shape))])
    return loudness


def deal_out(key, own, number, rows, count, top, bound, skew):
    ranking = jax.random.permutation(key, count)
    heavy_load, common = load_shares(count, rows * top, bound, skew, True), load_shares(count, rows * top, bound, skew, False)
    places = jnp.arange(count)

    def named(sizes, offset_by):
        used = int((sizes > 0).sum())
        fixed = max(1, used // 4)
        passed = fixed + (places - fixed + offset_by * (used - fixed)) % max(1, count - fixed)
        return jnp.zeros((count,), jnp.int32).at[ranking[jnp.where(places < fixed, places, passed)]].set(jnp.asarray(sizes, jnp.int32))

    sizes = jnp.where(number % 4 == 0, named(heavy_load, number // 4), named(common, number - number // 4 - 1))
    mixed = jax.random.permutation(jax.random.fold_in(own, 3), count)
    giver, sink = mixed[0:count // 2 * 2:2], mixed[1:count // 2 * 2:2]
    room = jnp.minimum(sizes[giver] - 1, bound - sizes[sink]) // 2
    room = jnp.where((giver == ranking[0]) | (sink == ranking[0]) | (sizes[sink] == 0), 0, jnp.maximum(room, 0))
    passed = jax.random.randint(jax.random.fold_in(own, 4), (count // 2,), 0, 1 << 20) % (room + 1)
    sizes = sizes.at[giver].add(-passed).at[sink].add(passed)
    items = jnp.searchsorted(jnp.cumsum(sizes), jnp.arange(rows * top), side="right").astype(jnp.int32)
    grid = items.reshape(top, rows).T
    grid = grid[jax.random.permutation(jax.random.fold_in(own, 1), rows)]
    offset_by = jax.random.randint(jax.random.fold_in(own, 2), (rows, 1), 0, top)
    return jnp.take_along_axis(grid, (jnp.arange(top)[None, :] + offset_by) % top, axis=1)


def load_shares(number_of, total, reach, skew, full):
    weights = [(1 << 20) // math.isqrt(grade ** skew) + 1 for grade in range(1, number_of + 1)]
    largest = reach if full else min(reach, max(-(-total // number_of), total * weights[0] // sum(weights)))
    least = 1 if total - largest >= number_of - 1 else 0
    counts, surplus = [largest] + [least] * (number_of - 1), total - largest - least * (number_of - 1)
    while surplus > 0:
        free = [i for i in range(1, number_of) if counts[i] < largest] or [i for i in range(1, number_of) if counts[i] < reach]
        pool, budget = sum([weights[i] for i in free]), surplus
        for i in free:
            extra = min(reach - counts[i], max(1, budget * weights[i] // pool), surplus)
            counts[i] = counts[i] + extra
            surplus = surplus - extra
    return np.array(counts)


def gaussian(stream_key, dims, width, reach, split=(), kind=jnp.bfloat16):
    array = jax.random.normal(stream_key, dims, jnp.float32) * width
    if len(split) > 0:
        array = levels(stream_key, dims, split, -0.22, 0.18) * array
    return jnp.clip(array, min=-reach, max=reach).astype(kind)


def setup_inputs(seed: int = 0, part: int = 0) -> dict:
    key_of = jax.random.split(jax.random.key(seed), 5)
    part_keys = jax.random.split(jax.random.fold_in(key_of[4], part), 5)
    embeddings = gaussian(part_keys[0], (ROWS, D), 1.0, 6.0, ((0, 16),))
    coarse_lists_keys = jax.random.split(jax.random.fold_in(part_keys[1], 1), ROWS // ROW_DEV)
    coarse_lists_turns = jax.random.permutation(jax.random.fold_in(part_keys[1], 3), ROWS // ROW_DEV)
    coarse_lists = jax.vmap(lambda own, number: deal_out(jax.random.fold_in(part_keys[1], 2), own, number, ROW_DEV, COARSE, TOP, MOST, 2))(coarse_lists_keys, coarse_lists_turns).reshape((ROWS, TOP))
    coarse_table = gaussian(key_of[2], (COARSE, D), 1.0, 6.0)
    fine_table = gaussian(key_of[3], (FINE, D), 1.0, 6.0, ((0, 16),))
    return {"embeddings": embeddings, "coarse_lists": coarse_lists, "coarse_table": coarse_table, "fine_table": fine_table}


def reference(embeddings, coarse_lists, coarse_table, fine_table):
    rows_all = embeddings.shape[0]
    coarse_all = coarse_table.shape[0]
    fine_all = fine_table.shape[0]
    factor = 1.0 / math.sqrt(D)
    group_size = math.gcd(rows_all, 64)
    group_count = rows_all // group_size
    coarse_wide = coarse_table.astype(jnp.float32)
    coarse_norm = lax.optimization_barrier(jnp.sum(coarse_wide * coarse_wide, -1))
    log_weights = jnp.full((coarse_all,), -math.log(coarse_all), jnp.float32)
    fine_state = fine_table.astype(jnp.float32)
    offsets = jnp.arange(FINE_PER, dtype=jnp.int32)
    grouped = (embeddings.reshape(group_count, group_size, D), coarse_lists.reshape(group_count, group_size, TOP))
    row_cost = jnp.zeros((rows_all,), jnp.float32)
    for iteration in range(ITERS):
        fine_bf = fine_state.astype(jnp.bfloat16)
        fine_wide = fine_bf.astype(jnp.float32)
        fine_norm = lax.optimization_barrier(jnp.sum(fine_wide * fine_wide, -1))

        def visit_block(totals, pieces):
            masses, stat_sums, fine_mass = totals
            block_rows, chosen = pieces
            rows_wide = block_rows.astype(jnp.float32)
            coarse_dots = jnp.dot(block_rows, coarse_table.T, preferred_element_type=jnp.float32)
            coarse_prob = jax.nn.softmax((coarse_dots - 0.5 * coarse_norm) * factor + log_weights, -1)
            listed = jnp.take_along_axis(coarse_prob, chosen, 1)
            coarse_resp = (listed / lax.optimization_barrier(jnp.sum(listed, -1, keepdims=True))).astype(jnp.bfloat16)
            resp_wide = coarse_resp.astype(jnp.float32)
            fine_index = (chosen[:, :, None] * FINE_PER + offsets).astype(jnp.int32)
            centers = fine_wide[fine_index]
            products = jnp.einsum('bd,btjd->btj', rows_wide, centers, precision=lax.Precision.HIGHEST)
            chosen_norm = fine_norm[fine_index]
            shares = jax.nn.softmax((products - 0.5 * chosen_norm) * factor, -1)
            weight = lax.optimization_barrier((resp_wide[:, :, None] * shares).astype(jnp.bfloat16)).astype(jnp.float32)
            row_norm = lax.optimization_barrier(jnp.sum(rows_wide * rows_wide, -1))
            distance = row_norm[:, None, None] - 2.0 * products + chosen_norm
            slot_cost = resp_wide * lax.optimization_barrier(jnp.sum(shares * distance, -1)) / D
            flat_index = fine_index.reshape(-1)
            fine_mass = fine_mass.at[flat_index].add(weight.reshape(-1))
            stat_sums = stat_sums.at[flat_index].add((weight[..., None] * rows_wide[:, None, None, :]).reshape(-1, D))
            masses = masses + lax.optimization_barrier(jnp.sum(coarse_prob, 0))
            return ((masses, stat_sums, fine_mass), lax.optimization_barrier(jnp.sum(slot_cost, -1)))
        start = (jnp.zeros((coarse_all,), jnp.float32), jnp.zeros((fine_all, D), jnp.float32), jnp.zeros((fine_all,), jnp.float32))
        (masses, stat_sums, fine_mass), costs = lax.scan(visit_block, start, grouped)
        fine_state = (stat_sums + fine_state) / (fine_mass + 1.0)[:, None]
        log_weights = jnp.log((masses + 1.0) / (rows_all + coarse_all))
        row_cost = costs.reshape(rows_all)
    return (fine_state.astype(jnp.bfloat16), row_cost, log_weights)
```

```python
import math

import functools

import jax
import jax.numpy as jnp
from jax import lax
from jax.experimental import pallas as pl
from jax.experimental.pallas import tpu as pltpu
from jax.sharding import PartitionSpec as P

FINE_PER = 64
TOP = 8
ITERS = 2


def dispatch_body(embeddings, coarse_lists, coarse_table, fine_table):
    local_rows, model_width = embeddings.shape
    coarse_all = coarse_table.shape[0]
    clusters_dev = fine_table.shape[0] // FINE_PER
    cent_size = lax.axis_size("cent")
    rest_size = lax.axis_size(("rows", "sub"))
    devices = lax.axis_size(("cent", "rows", "sub"))
    rows_all = local_rows * devices
    most_rows = max(2, 2 * local_rows * TOP // coarse_all)
    factor = 1.0 / math.sqrt(model_width)
    slot_total = coarse_all * most_rows
    received = devices * most_rows
    coarse_norm = jnp.einsum(
        "kd,kd->k", coarse_table, coarse_table, preferred_element_type=jnp.float32
    )
    flat_ids = coarse_lists.reshape(-1)
    copies = flat_ids.shape[0]
    order_ids = jnp.argsort(flat_ids, stable=True)
    sorted_ids = flat_ids[order_ids]
    first_seen = jnp.searchsorted(sorted_ids, sorted_ids, side="left")
    sorted_position = jnp.arange(copies, dtype=jnp.int32) - first_seen
    position = jnp.zeros((copies,), jnp.int32).at[order_ids].set(sorted_position)
    slot_index = flat_ids * most_rows + position
    copy_rows = jnp.arange(copies, dtype=jnp.int32) // TOP
    source_row = jnp.full((slot_total,), -1, jnp.int32).at[slot_index].set(copy_rows)
    filled = source_row >= 0
    picked = embeddings[jnp.maximum(source_row, 0)]
    row_buffer = jnp.where(filled[:, None], picked, jnp.zeros_like(picked))
    row_buffer = row_buffer.reshape(cent_size, rest_size, clusters_dev, most_rows * model_width)
    log_weights = jnp.full((coarse_all,), -math.log(coarse_all), jnp.float32)
    fine_state = fine_table.astype(jnp.float32)
    row_cost = jnp.zeros((local_rows,), jnp.float32)
    got_rows = lax.all_to_all(
        lax.all_to_all(row_buffer, "cent", split_axis=0, concat_axis=3, tiled=True),
        ("rows", "sub"),
        split_axis=1,
        concat_axis=3,
        tiled=True,
    )
    for iteration in range(ITERS):
        coarse_dots = jnp.einsum(
            "rd,kd->rk", embeddings, coarse_table, preferred_element_type=jnp.float32
        )
        coarse_prob = jax.nn.softmax((coarse_dots - 0.5 * coarse_norm) * factor + log_weights, -1)
        masses = lax.psum(jnp.sum(coarse_prob, 0), ("cent", "rows", "sub"))
        listed = jnp.take_along_axis(coarse_prob, coarse_lists, 1)
        coarse_resp = (listed / jnp.sum(listed, -1, keepdims=True)).astype(jnp.bfloat16)
        resp_buffer = (
            jnp.zeros((slot_total,), jnp.bfloat16).at[slot_index].set(coarse_resp.reshape(-1))
        )
        resp_buffer = resp_buffer.reshape(cent_size, rest_size, clusters_dev, most_rows)
        got_resp = lax.all_to_all(
            lax.all_to_all(resp_buffer, "cent", split_axis=0, concat_axis=3, tiled=True),
            ("rows", "sub"),
            split_axis=1,
            concat_axis=3,
            tiled=True,
        )
        fine_bf = fine_state.astype(jnp.bfloat16)
        fine_norm = jnp.sum(jnp.square(fine_bf.astype(jnp.float32)), -1).reshape(
            clusters_dev, FINE_PER
        )
        slab_rows = got_rows.reshape(clusters_dev, received, model_width)
        slab_resp = got_resp.reshape(clusters_dev, received).astype(jnp.float32)
        centers = fine_bf.reshape(clusters_dev, FINE_PER, model_width)
        products = jnp.einsum(
            "cjd,csd->cjs", centers, slab_rows, preferred_element_type=jnp.float32
        )
        norm_term = fine_norm[:, :, None]
        shares = jax.nn.softmax((products - 0.5 * norm_term) * factor, 1)
        weight = (slab_resp[:, None, :] * shares).astype(jnp.bfloat16)
        fine_mass = jnp.sum(weight.astype(jnp.float32), 2).reshape(-1)
        stat_sums = jnp.einsum(
            "cjs,csd->cjd", weight, slab_rows, preferred_element_type=jnp.float32
        ).reshape(-1, model_width)
        if iteration == ITERS - 1:
            row_norm = jnp.einsum(
                "csd,csd->cs", slab_rows, slab_rows, preferred_element_type=jnp.float32
            )
            distance = row_norm[:, None, :] - 2.0 * products + norm_term
            slot_cost = slab_resp * jnp.sum(shares * distance, 1) / model_width
            slot_cost = slot_cost.reshape(1, 1, clusters_dev, rest_size, cent_size * most_rows)
            returned = lax.all_to_all(
                lax.all_to_all(slot_cost, "cent", split_axis=4, concat_axis=0, tiled=True),
                ("rows", "sub"),
                split_axis=3,
                concat_axis=1,
                tiled=True,
            )
            row_cost = jnp.sum(returned.reshape(-1)[slot_index].reshape(local_rows, TOP), -1)
        fine_state = (stat_sums + fine_state) / (fine_mass + 1.0)[:, None]
        log_weights = jnp.log((masses + 1.0) / (rows_all + coarse_all))
    device_index = lax.axis_index(("cent", "rows", "sub"))
    own_weights = lax.dynamic_slice_in_dim(log_weights, device_index * clusters_dev, clusters_dev)
    return (fine_state.astype(jnp.bfloat16), row_cost, own_weights)


GATHER_MAX = 8 * 1024 * 1024
HALVES = 2
MESH = pl.DeviceIdType.MESH


def gather_kernel(
    cent_size,
    emb_ref,
    lists_ref,
    coarse_ref,
    fine_ref,
    fine_out_ref,
    cost_out_ref,
    weights_out_ref,
    rows_all_ref,
    lists_all_ref,
    logits_ref,
    prob_ref,
    mass_ref,
    fine_bf_ref,
    state_ref,
    half_norm_ref,
    products_ref,
    weight_ref,
    stats_ref,
    fine_mass_ref,
    log_weights_ref,
    resp_sum_ref,
    cost_part_ref,
    cost_got_ref,
    row_send,
    cross_send,
    twin_send,
    row_recv,
    lists_send,
    lists_recv,
    cost_send,
    cost_recv,
):
    local_rows, width = emb_ref.shape
    coarse_all = coarse_ref.shape[0]
    fine_dev = fine_ref.shape[0]
    clusters_dev = fine_dev // FINE_PER
    devices = 4 * cent_size
    chips = 2 * cent_size
    piece = local_rows // HALVES
    chunk_rows = 2 * local_rows
    factor = 1.0 / math.sqrt(width)
    group = lax.axis_index("groups")
    z = lax.axis_index("cent")
    x = lax.axis_index("rows")
    s = lax.axis_index("sub")
    me = (z * 2 + x) * 2 + s
    f32 = jnp.float32

    def device(index):
        return (group, index // 4, (index // 2) % 2, index % 2)

    barrier = pltpu.get_barrier_semaphore()

    def greet(step, carry):
        other = lax.rem(me + step, devices)
        pl.semaphore_signal(barrier, inc=1, device_id=device(other), device_id_type=MESH)
        return carry

    lax.fori_loop(1, devices, greet, 0)
    pl.semaphore_wait(barrier, devices - 1)

    def slot(zz, xx, ss, half):
        return ((zz * 2 + xx) * 2 + ss) * HALVES + half

    def copy_rows(src, index, sem, target):
        return pltpu.make_async_remote_copy(
            src_ref=src,
            dst_ref=rows_all_ref.at[index],
            send_sem=sem,
            recv_sem=row_recv.at[index],
            device_id=target,
            device_id_type=MESH,
        )

    def to_right(src, zz, half):
        return copy_rows(src, slot(zz, x, s, half), row_send.at[0, zz, half], (group, z + 1, x, s))

    def to_left(src, zz, half):
        return copy_rows(src, slot(zz, x, s, half), row_send.at[1, zz, half], (group, z - 1, x, s))

    def to_cross(src, zz, half):
        return copy_rows(src, slot(zz, x, s, half), cross_send.at[zz, half], (group, z, 1 - x, s))

    def to_twin(src, zz, xx, half):
        return copy_rows(
            src, slot(zz, xx, s, half), twin_send.at[zz, xx, half], (group, z, x, 1 - s)
        )

    def held(zz, xx, half):
        return rows_all_ref.at[slot(zz, xx, s, half)]

    def wait_rows(index):
        copy_rows(rows_all_ref.at[index], index, twin_send.at[0, 0, 0], (group, z, x, 1 - s)).wait_recv()

    for half in range(HALVES):
        mine = emb_ref.at[pl.ds(half * piece, piece)]

        @pl.when(z + 1 < cent_size)
        def _():
            to_right(mine, z, half).start()

        @pl.when(z >= 1)
        def _():
            to_left(mine, z, half).start()

        to_cross(mine, z, half).start()
        to_twin(mine, z, x, half).start()

    lists = lists_ref[...].astype(f32)
    lane = lax.broadcasted_iota(jnp.int32, (local_rows, 128), 1)
    wide = jnp.zeros((local_rows, 128), f32)
    for t in range(TOP):
        wide = jnp.where(lane == t, lists[:, t : t + 1], wide)
    lists_all_ref[me] = jnp.transpose(wide)[:TOP].astype(jnp.int32)

    def copy_lists(owner, other):
        return pltpu.make_async_remote_copy(
            src_ref=lists_all_ref.at[owner],
            dst_ref=lists_all_ref.at[owner],
            send_sem=lists_send.at[other],
            recv_sem=lists_recv.at[owner],
            device_id=device(other),
            device_id_type=MESH,
        )

    def send_lists(step, carry):
        copy_lists(me, lax.rem(me + step, devices)).start()
        return carry

    lax.fori_loop(1, devices, send_lists, 0)

    for half in range(HALVES):
        rows_all_ref[slot(z, x, s, half)] = emb_ref[pl.ds(half * piece, piece), :]
    own_wide = emb_ref[...].astype(f32)
    row_norm = jnp.sum(own_wide * own_wide, axis=1, keepdims=True)
    row_norm = jnp.transpose(jnp.broadcast_to(row_norm, (local_rows, 128)))[0:1, :]

    coarse_wide = coarse_ref[...].astype(f32)
    coarse_half = 0.5 * jnp.sum(coarse_wide * coarse_wide, axis=1, keepdims=True)
    fine_bf_ref[...] = fine_ref[...]
    mass_ref[...] = jnp.zeros_like(mass_ref)
    log_weights_ref[...] = jnp.full(log_weights_ref.shape, -math.log(coarse_all), f32)

    def begin_iteration():
        fine_wide = fine_bf_ref[...].astype(f32)
        half_norm_ref[...] = jnp.broadcast_to(
            0.5 * jnp.sum(fine_wide * fine_wide, axis=1, keepdims=True), half_norm_ref.shape
        )
        stats_ref[...] = jnp.zeros_like(stats_ref)
        fine_mass_ref[...] = jnp.zeros_like(fine_mass_ref)

    begin_iteration()
    dims = (((1,), (1,)), ((), ()))
    ones = jnp.ones((chunk_rows, 128), jnp.bfloat16)

    def visit(chip, last):
        base = chip * (2 * HALVES)
        rows = rows_all_ref[pl.ds(base, 2 * HALVES)].reshape(chunk_rows, width)
        if last:
            logits = logits_ref[chip]
        else:
            dots = lax.dot_general(coarse_ref[...], rows, dims, preferred_element_type=f32)
            logits = (dots - coarse_half) * factor
            logits_ref[chip] = logits
        products_ref[...] = lax.dot_general(
            fine_bf_ref[...], rows, dims, preferred_element_type=f32
        )
        logits = logits + log_weights_ref[:, 0:1]
        raised = jnp.exp(logits - jnp.max(logits, axis=0, keepdims=True))
        prob = raised * (1.0 / jnp.sum(raised, axis=0, keepdims=True))
        mass_ref[...] += prob[:, :128] + prob[:, 128:]
        cluster = lax.broadcasted_iota(jnp.int32, (coarse_all, local_rows), 0)
        masks = []
        for core in range(2):
            named = lists_all_ref[chip * 2 + core]
            mask = cluster == named[0:1, :]
            for t in range(1, TOP):
                mask = jnp.logical_or(mask, cluster == named[t : t + 1, :])
            masks.append(jnp.where(mask, prob[:, core * local_rows : (core + 1) * local_rows], 0.0))
        listed = jnp.concatenate(masks, axis=1)
        resp = listed / jnp.sum(listed, axis=0, keepdims=True)
        resp = resp.astype(jnp.bfloat16).astype(f32)
        prob_ref[...] = resp
        if last:
            resp_sum_ref[chip] = jnp.sum(resp, axis=0, keepdims=True)
        own = prob_ref[pl.ds(pl.multiple_of(me * clusters_dev, clusters_dev), clusters_dev), :]
        cost = jnp.zeros((1, chunk_rows), f32)
        for k in range(clusters_dev):
            span = pl.ds(k * FINE_PER, FINE_PER)
            norm = half_norm_ref[span, :]
            norm = jnp.concatenate([norm, norm], axis=1)
            score = (products_ref[span, :] - norm) * factor
            score_max = jnp.max(score, axis=0, keepdims=True)
            grown = jnp.exp(score - score_max)
            share_scale = own[k : k + 1, :] / jnp.sum(grown, axis=0, keepdims=True)
            weight_ref[span, :] = (grown * share_scale).astype(jnp.bfloat16)
            if last:
                cost = cost + share_scale * jnp.sum(grown * score, axis=0, keepdims=True)
        weight = weight_ref[...]
        stats_ref[...] += lax.dot_general(
            weight, rows, (((1,), (0,)), ((), ())), preferred_element_type=f32
        )
        fine_mass_ref[...] += lax.dot_general(
            weight, ones, (((1,), (0,)), ((), ())), preferred_element_type=f32
        )
        if last:
            cost = cost * (-2.0 / (factor * width))
            for core in range(2):
                cost_part_ref[chip * 2 + core] = cost[:, core * local_rows : (core + 1) * local_rows]

    def spread(step, carry):
        for half in range(HALVES):
            left_z, right_z = z - step - 1, z + step + 1

            @pl.when(left_z >= 0)
            def _():
                wait_rows(slot(left_z, x, s, half))

                @pl.when(z + 1 < cent_size)
                def _():
                    to_right(held(left_z, x, half), left_z, half).start()

                to_cross(held(left_z, x, half), left_z, half).start()
                to_twin(held(left_z, x, half), left_z, x, half).start()

            @pl.when(right_z < cent_size)
            def _():
                wait_rows(slot(right_z, x, s, half))

                @pl.when(z >= 1)
                def _():
                    to_left(held(right_z, x, half), right_z, half).start()

                to_cross(held(right_z, x, half), right_z, half).start()
                to_twin(held(right_z, x, half), right_z, x, half).start()

        def crossed(side, carry):
            zz = z - step + 2 * step * side
            there = jnp.logical_and(zz >= 0, zz < cent_size)

            @pl.when(jnp.logical_and(there, step + 1 > side))
            def _():
                for half in range(HALVES):
                    wait_rows(slot(zz, 1 - x, s, half))
                    to_twin(held(zz, 1 - x, half), zz, 1 - x, half).start()

            return carry

        def computed(turn, carry):
            side = turn // 2
            zz = z - step + 2 * step * side
            xx = lax.rem(x + turn, 2)
            there = jnp.logical_and(zz >= 0, zz < cent_size)

            @pl.when(jnp.logical_and(there, step + 1 > side))
            def _():
                chip = zz * 2 + xx
                for half in range(HALVES):
                    wait_rows(slot(zz, xx, 1 - s, half))
                for core in range(2):

                    @pl.when(chip * 2 + core != me)
                    def _():
                        copy_lists(chip * 2 + core, lax.rem(me + 1, devices)).wait_recv()

                visit(chip, False)

            return carry

        lax.fori_loop(0, 2, crossed, 0)
        lax.fori_loop(0, 4, computed, 0)
        return carry

    lax.fori_loop(0, cent_size, spread, 0)

    def new_state(previous):
        scale = 1.0 / (fine_mass_ref[...] + 1.0)
        scale = jnp.concatenate([scale] * (width // 128), axis=1)
        return (stats_ref[...] + previous) * scale

    def new_log_weights():
        total = jnp.sum(mass_ref[...], axis=1, keepdims=True)
        fresh = jnp.log((total + 1.0) / (devices * local_rows + coarse_all))
        log_weights_ref[...] = jnp.broadcast_to(fresh, log_weights_ref.shape)
        mass_ref[...] = jnp.zeros_like(mass_ref)

    state = new_state(fine_ref[...].astype(f32))
    state_ref[...] = state
    fine_bf_ref[...] = state.astype(jnp.bfloat16)
    new_log_weights()
    begin_iteration()

    def copy_cost(owner, other):
        return pltpu.make_async_remote_copy(
            src_ref=cost_part_ref.at[other],
            dst_ref=cost_got_ref.at[owner],
            send_sem=cost_send.at[other],
            recv_sem=cost_recv.at[owner],
            device_id=device(other),
            device_id_type=MESH,
        )

    def second(step, carry):
        chip = lax.rem(z * 2 + x + step, chips)
        visit(chip, True)
        for core in range(2):

            @pl.when(chip * 2 + core != me)
            def _():
                copy_cost(me, chip * 2 + core).start()

        return carry

    lax.fori_loop(1, chips + 1, second, 0)

    fine_out_ref[...] = new_state(state_ref[...]).astype(jnp.bfloat16)
    new_log_weights()
    own_weights = log_weights_ref[
        pl.ds(pl.multiple_of(me * clusters_dev, clusters_dev), clusters_dev), :
    ]
    diagonal = lax.broadcasted_iota(jnp.int32, own_weights.shape, 0) == lax.broadcasted_iota(
        jnp.int32, own_weights.shape, 1
    )
    own_weights = jnp.sum(jnp.where(diagonal, own_weights, 0.0), axis=0, keepdims=True)
    weights_out_ref[...] = own_weights[:, :clusters_dev]

    def drain(step, carry):
        other = lax.rem(me + step, devices)
        copy_lists(me, other).wait_send()
        copy_cost(me, other).wait_send()
        return carry

    lax.fori_loop(1, devices, drain, 0)

    def drain_rows(zz, carry):
        for half in range(HALVES):

            @pl.when(jnp.logical_and(z + 1 < cent_size, zz <= z))
            def _():
                to_right(held(zz, x, half), zz, half).wait_send()

            @pl.when(jnp.logical_and(z >= 1, zz >= z))
            def _():
                to_left(held(zz, x, half), zz, half).wait_send()

            to_cross(held(zz, x, half), zz, half).wait_send()
            for xx in range(2):
                to_twin(held(zz, xx, half), zz, xx, half).wait_send()
        return carry

    lax.fori_loop(0, cent_size, drain_rows, 0)

    resp_sum = resp_sum_ref[z * 2 + x]
    resp_sum = jnp.where(s == 0, resp_sum[:, :local_rows], resp_sum[:, local_rows:])
    total = row_norm * resp_sum * (1.0 / width) + cost_part_ref[me]

    def collect(step, total):
        other = lax.rem(me + step, devices)
        copy_cost(other, other).wait_recv()
        return total + cost_got_ref[other]

    cost_out_ref[...] = lax.fori_loop(1, devices, collect, total)


def gather_body(cent_size, embeddings, coarse_lists, coarse_table, fine_table):
    local_rows, width = embeddings.shape
    coarse_all = coarse_table.shape[0]
    fine_dev = fine_table.shape[0]
    clusters_dev = fine_dev // FINE_PER
    devices = 4 * cent_size
    chips = 2 * cent_size
    chunk = 2 * local_rows
    f32, bf16 = jnp.float32, jnp.bfloat16
    dma = pltpu.SemaphoreType.DMA
    fine_out, row_cost, own_weights = pl.pallas_call(
        functools.partial(gather_kernel, cent_size),
        out_shape=(
            jax.ShapeDtypeStruct((fine_dev, width), bf16),
            jax.ShapeDtypeStruct((1, local_rows), f32),
            jax.ShapeDtypeStruct((1, clusters_dev), f32),
        ),
        in_specs=[pl.BlockSpec(memory_space=pltpu.VMEM)] * 4,
        out_specs=(pl.BlockSpec(memory_space=pltpu.VMEM),) * 3,
        scratch_shapes=[
            pltpu.VMEM((devices * HALVES, local_rows // HALVES, width), bf16),
            pltpu.VMEM((devices, TOP, local_rows), jnp.int32),
            pltpu.VMEM((chips, coarse_all, chunk), f32),
            pltpu.VMEM((coarse_all, chunk), f32),
            pltpu.VMEM((coarse_all, 128), f32),
            pltpu.VMEM((fine_dev, width), bf16),
            pltpu.VMEM((fine_dev, width), f32),
            pltpu.VMEM((fine_dev, 128), f32),
            pltpu.VMEM((fine_dev, chunk), f32),
            pltpu.VMEM((fine_dev, chunk), bf16),
            pltpu.VMEM((fine_dev, width), f32),
            pltpu.VMEM((fine_dev, 128), f32),
            pltpu.VMEM((coarse_all, 128), f32),
            pltpu.VMEM((chips, 1, chunk), f32),
            pltpu.VMEM((devices, 1, local_rows), f32),
            pltpu.VMEM((devices, 1, local_rows), f32),
            dma((2, cent_size, HALVES)),
            dma((cent_size, HALVES)),
            dma((cent_size, 2, HALVES)),
            dma((devices * HALVES,)),
            dma((devices,)),
            dma((devices,)),
            dma((devices,)),
            dma((devices,)),
        ],
        compiler_params=pltpu.CompilerParams(
            collective_id=0, has_side_effects=True, vmem_limit_bytes=40 * 1024 * 1024
        ),
    )(embeddings, coarse_lists, coarse_table, fine_table)
    return fine_out, row_cost.reshape(-1), own_weights.reshape(-1)


def solution(mesh):
    sizes = dict(mesh.shape)

    def body(embeddings, coarse_lists, coarse_table, fine_table):
        devices = sizes["cent"] * sizes["rows"] * sizes["sub"]
        gathered_bytes = 2 * devices * embeddings.size
        fits = gathered_bytes <= GATHER_MAX and embeddings.shape[0] == 128
        fits = fits and fine_table.shape[0] == 8 * FINE_PER
        if sizes["rows"] == 2 and sizes["sub"] == 2 and fits:
            return gather_body(sizes["cent"], embeddings, coarse_lists, coarse_table, fine_table)
        return dispatch_body(embeddings, coarse_lists, coarse_table, fine_table)

    return jax.shard_map(
        body,
        mesh=mesh,
        in_specs=(
            P(("groups", "cent", "rows", "sub"), None),
            P(("groups", "cent", "rows", "sub"), None),
            P(),
            P(("cent", "rows", "sub"), None),
        ),
        out_specs=(
            P(("groups", "cent", "rows", "sub"), None),
            P(("groups", "cent", "rows", "sub")),
            P(("groups", "cent", "rows", "sub")),
        ),
        check_vma=False,
    )
```

```python
import math

import functools

import jax
import jax.numpy as jnp
from jax import lax
from jax.experimental import pallas as pl
from jax.experimental.pallas import tpu as pltpu
from jax.sharding import PartitionSpec as P

FINE_PER = 64
TOP = 8
ITERS = 2


def dispatch_body(embeddings, coarse_lists, coarse_table, fine_table):
    local_rows, model_width = embeddings.shape
    coarse_all = coarse_table.shape[0]
    clusters_dev = fine_table.shape[0] // FINE_PER
    cent_size = lax.axis_size("cent")
    rest_size = lax.axis_size(("rows", "sub"))
    devices = lax.axis_size(("cent", "rows", "sub"))
    rows_all = local_rows * devices
    most_rows = max(2, 2 * local_rows * TOP // coarse_all)
    factor = 1.0 / math.sqrt(model_width)
    slot_total = coarse_all * most_rows
    received = devices * most_rows
    coarse_norm = jnp.einsum(
        "kd,kd->k", coarse_table, coarse_table, preferred_element_type=jnp.float32
    )
    flat_ids = coarse_lists.reshape(-1)
    copies = flat_ids.shape[0]
    order_ids = jnp.argsort(flat_ids, stable=True)
    sorted_ids = flat_ids[order_ids]
    first_seen = jnp.searchsorted(sorted_ids, sorted_ids, side="left")
    sorted_position = jnp.arange(copies, dtype=jnp.int32) - first_seen
    position = jnp.zeros((copies,), jnp.int32).at[order_ids].set(sorted_position)
    slot_index = flat_ids * most_rows + position
    copy_rows = jnp.arange(copies, dtype=jnp.int32) // TOP
    source_row = jnp.full((slot_total,), -1, jnp.int32).at[slot_index].set(copy_rows)
    filled = source_row >= 0
    picked = embeddings[jnp.maximum(source_row, 0)]
    row_buffer = jnp.where(filled[:, None], picked, jnp.zeros_like(picked))
    row_buffer = row_buffer.reshape(cent_size, rest_size, clusters_dev, most_rows * model_width)
    log_weights = jnp.full((coarse_all,), -math.log(coarse_all), jnp.float32)
    fine_state = fine_table.astype(jnp.float32)
    row_cost = jnp.zeros((local_rows,), jnp.float32)
    got_rows = lax.all_to_all(
        lax.all_to_all(row_buffer, "cent", split_axis=0, concat_axis=3, tiled=True),
        ("rows", "sub"),
        split_axis=1,
        concat_axis=3,
        tiled=True,
    )
    for iteration in range(ITERS):
        coarse_dots = jnp.einsum(
            "rd,kd->rk", embeddings, coarse_table, preferred_element_type=jnp.float32
        )
        coarse_prob = jax.nn.softmax((coarse_dots - 0.5 * coarse_norm) * factor + log_weights, -1)
        masses = lax.psum(jnp.sum(coarse_prob, 0), ("cent", "rows", "sub"))
        listed = jnp.take_along_axis(coarse_prob, coarse_lists, 1)
        coarse_resp = (listed / jnp.sum(listed, -1, keepdims=True)).astype(jnp.bfloat16)
        resp_buffer = (
            jnp.zeros((slot_total,), jnp.bfloat16).at[slot_index].set(coarse_resp.reshape(-1))
        )
        resp_buffer = resp_buffer.reshape(cent_size, rest_size, clusters_dev, most_rows)
        got_resp = lax.all_to_all(
            lax.all_to_all(resp_buffer, "cent", split_axis=0, concat_axis=3, tiled=True),
            ("rows", "sub"),
            split_axis=1,
            concat_axis=3,
            tiled=True,
        )
        fine_bf = fine_state.astype(jnp.bfloat16)
        fine_norm = jnp.sum(jnp.square(fine_bf.astype(jnp.float32)), -1).reshape(
            clusters_dev, FINE_PER
        )
        slab_rows = got_rows.reshape(clusters_dev, received, model_width)
        slab_resp = got_resp.reshape(clusters_dev, received).astype(jnp.float32)
        centers = fine_bf.reshape(clusters_dev, FINE_PER, model_width)
        products = jnp.einsum(
            "cjd,csd->cjs", centers, slab_rows, preferred_element_type=jnp.float32
        )
        norm_term = fine_norm[:, :, None]
        shares = jax.nn.softmax((products - 0.5 * norm_term) * factor, 1)
        weight = (slab_resp[:, None, :] * shares).astype(jnp.bfloat16)
        fine_mass = jnp.sum(weight.astype(jnp.float32), 2).reshape(-1)
        stat_sums = jnp.einsum(
            "cjs,csd->cjd", weight, slab_rows, preferred_element_type=jnp.float32
        ).reshape(-1, model_width)
        if iteration == ITERS - 1:
            row_norm = jnp.einsum(
                "csd,csd->cs", slab_rows, slab_rows, preferred_element_type=jnp.float32
            )
            distance = row_norm[:, None, :] - 2.0 * products + norm_term
            slot_cost = slab_resp * jnp.sum(shares * distance, 1) / model_width
            slot_cost = slot_cost.reshape(1, 1, clusters_dev, rest_size, cent_size * most_rows)
            returned = lax.all_to_all(
                lax.all_to_all(slot_cost, "cent", split_axis=4, concat_axis=0, tiled=True),
                ("rows", "sub"),
                split_axis=3,
                concat_axis=1,
                tiled=True,
            )
            row_cost = jnp.sum(returned.reshape(-1)[slot_index].reshape(local_rows, TOP), -1)
        fine_state = (stat_sums + fine_state) / (fine_mass + 1.0)[:, None]
        log_weights = jnp.log((masses + 1.0) / (rows_all + coarse_all))
    device_index = lax.axis_index(("cent", "rows", "sub"))
    own_weights = lax.dynamic_slice_in_dim(log_weights, device_index * clusters_dev, clusters_dev)
    return (fine_state.astype(jnp.bfloat16), row_cost, own_weights)


GATHER_MAX = 8 * 1024 * 1024
SPANS = ((0, 64), (64, 48), (112, 16))
LATE = len(SPANS) - 1
MESH = pl.DeviceIdType.MESH


def gather_kernel(
    cent_size,
    emb_ref,
    lists_ref,
    coarse_hbm_ref,
    fine_hbm_ref,
    fine_out_ref,
    cost_out_ref,
    weights_out_ref,
    coarse_ref,
    rows_all_ref,
    lists_all_ref,
    logits_ref,
    prob_ref,
    mask_ref,
    mass_ref,
    fine_bf_ref,
    half_norm_ref,
    products_ref,
    weight_ref,
    stats_ref,
    fine_mass_ref,
    log_weights_ref,
    cost_part_ref,
    cost_got_ref,
    load_sem,
    row_send,
    cross_send,
    twin_send,
    row_recv,
    lists_send,
    lists_recv,
    cost_send,
    cost_recv,
):
    local_rows, width = emb_ref.shape
    coarse_all = coarse_ref.shape[0]
    fine_dev = fine_bf_ref.shape[0]
    clusters_dev = fine_dev // FINE_PER
    devices = 4 * cent_size
    chips = 2 * cent_size
    chunk_rows = 2 * local_rows
    factor = 1.0 / math.sqrt(width)
    group = lax.axis_index("groups")
    z = lax.axis_index("cent")
    x = lax.axis_index("rows")
    s = lax.axis_index("sub")
    me = (z * 2 + x) * 2 + s
    f32 = jnp.float32

    def device(index):
        return (group, index // 4, (index // 2) % 2, index % 2)

    own_rows = rows_all_ref.at[pl.ds(pl.multiple_of(me * local_rows, local_rows), local_rows)]
    load_rows = pltpu.make_async_copy(emb_ref, own_rows, load_sem.at[0])
    load_lists = pltpu.make_async_copy(lists_ref, lists_all_ref.at[me], load_sem.at[1])
    load_coarse = pltpu.make_async_copy(coarse_hbm_ref, coarse_ref, load_sem.at[2])
    load_fine = pltpu.make_async_copy(fine_hbm_ref, fine_bf_ref, load_sem.at[3])
    load_rows.start()
    load_lists.start()
    load_coarse.start()
    load_fine.start()

    barrier = pltpu.get_barrier_semaphore()

    def greet(step, carry):
        other = lax.rem(me + step, devices)
        pl.semaphore_signal(barrier, inc=1, device_id=device(other), device_id_type=MESH)
        return carry

    lax.fori_loop(1, devices, greet, 0)
    pl.semaphore_wait(barrier, devices - 1)

    def copy_rows(zz, xx, ss, span, sem, target):
        owner = (zz * 2 + xx) * 2 + ss
        start, count = SPANS[span]
        place = rows_all_ref.at[pl.ds(pl.multiple_of(owner * local_rows + start, 16), count)]
        return pltpu.make_async_remote_copy(
            src_ref=place,
            dst_ref=place,
            send_sem=sem,
            recv_sem=row_recv.at[owner, span],
            device_id=target,
            device_id_type=MESH,
        )

    def to_right(zz, xx, span, way):
        return copy_rows(zz, xx, s, span, row_send.at[0, zz, way], (group, z + 1, x, s))

    def to_left(zz, xx, span, way):
        return copy_rows(zz, xx, s, span, row_send.at[1, zz, way], (group, z - 1, x, s))

    def to_cross(zz, span):
        return copy_rows(zz, x, s, span, cross_send.at[zz, span], (group, z, 1 - x, s))

    def to_twin(zz, xx, span):
        return copy_rows(zz, xx, s, span, twin_send.at[zz, xx, span], (group, z, x, 1 - s))

    def wait_rows(zz, xx, ss, span):
        copy_rows(zz, xx, ss, span, twin_send.at[0, 0, 0], (group, z, x, 1 - s)).wait_recv()

    def send_right(zz, xx, span, way):
        @pl.when(z + 1 < cent_size)
        def _():
            to_right(zz, xx, span, way).start()

    def send_left(zz, xx, span, way):
        @pl.when(z >= 1)
        def _():
            to_left(zz, xx, span, way).start()

    load_rows.wait()
    to_cross(z, LATE).start()
    for span in range(LATE):
        send_right(z, x, span, span)
        send_left(z, x, span, span)
        to_cross(z, span).start()
    send_right(z, x, LATE, LATE)
    send_left(z, x, LATE, LATE)
    for span in range(len(SPANS)):
        to_twin(z, x, span).start()
    load_lists.wait()

    def copy_lists(owner, other):
        return pltpu.make_async_remote_copy(
            src_ref=lists_all_ref.at[owner],
            dst_ref=lists_all_ref.at[owner],
            send_sem=lists_send.at[other],
            recv_sem=lists_recv.at[owner],
            device_id=device(other),
            device_id_type=MESH,
        )

    def send_lists(step, carry):
        copy_lists(me, lax.rem(me + step, devices)).start()
        return carry

    lax.fori_loop(1, devices, send_lists, 0)

    wait_rows(z, 1 - x, s, LATE)
    send_right(z, 1 - x, LATE, LATE + 1)
    send_left(z, 1 - x, LATE, LATE + 1)
    to_twin(z, 1 - x, LATE).start()

    load_coarse.wait()
    load_fine.wait()
    coarse_wide = coarse_ref[...].astype(f32)
    coarse_half = 0.5 * jnp.sum(coarse_wide * coarse_wide, axis=1, keepdims=True)
    mass_ref[...] = jnp.zeros_like(mass_ref)
    log_weights_ref[...] = jnp.full(log_weights_ref.shape, -math.log(coarse_all), f32)

    scale = factor * math.log2(math.e)

    def keep_norm(span, centers):
        wide = centers.astype(f32)
        norm = (0.5 * scale) * jnp.sum(wide * wide, axis=1, keepdims=True)
        half_norm_ref[span, :] = jnp.broadcast_to(norm, (FINE_PER, 128))

    spans = [pl.ds(k * FINE_PER, FINE_PER) for k in range(clusters_dev)]
    for span in spans:
        keep_norm(span, fine_bf_ref[span, :])
        stats_ref[span, :] = fine_bf_ref[span, :].astype(f32)
    fine_mass_ref[...] = jnp.zeros_like(fine_mass_ref)
    dims = (((1,), (1,)), ((), ()))
    plain = (((1,), (0,)), ((), ()))
    ones = jnp.ones((chunk_rows, 128), jnp.bfloat16)

    def rows_of(chip):
        return rows_all_ref[pl.ds(pl.multiple_of(chip * chunk_rows, chunk_rows), chunk_rows), :]

    def find_products(chip, buffer):
        products_ref[buffer] = lax.dot_general(
            fine_bf_ref[...], rows_of(chip), dims, preferred_element_type=f32
        )

    def find_logits(chip):
        dots = lax.dot_general(coarse_ref[...], rows_of(chip), dims, preferred_element_type=f32)
        logits_ref[chip] = (dots - coarse_half) * factor
        cluster = lax.broadcasted_iota(jnp.int32, (coarse_all, local_rows), 0)
        for core in range(2):
            named = lists_all_ref[chip * 2 + core]
            mask = cluster == named[0:1, :]
            for t in range(1, TOP):
                mask = jnp.logical_or(mask, cluster == named[t : t + 1, :])
            mask_ref[chip, :, core * local_rows : (core + 1) * local_rows] = mask.astype(f32)

    def find_resp(chip, buffer):
        logits = logits_ref[chip] + jnp.concatenate([log_weights_ref[...]] * 2, axis=1)
        raised = jnp.exp(logits - jnp.max(logits, axis=0, keepdims=True))
        prob = raised * (1.0 / jnp.sum(raised, axis=0, keepdims=True))
        mass_ref[...] += prob[:, :128] + prob[:, 128:]
        listed = mask_ref[chip] * prob
        prob_ref[buffer] = listed
        start = pl.multiple_of(me * clusters_dev, clusters_dev)
        own = prob_ref[buffer, pl.ds(start, clusters_dev), :]
        own = own / jnp.sum(listed, axis=0, keepdims=True)
        return own.astype(jnp.bfloat16).astype(f32)

    def find_weights(own, buffer, store, last):
        cost = jnp.zeros((1, chunk_rows), f32)
        for k, span in enumerate(spans):
            norm = half_norm_ref[span, :]
            score = products_ref[buffer, span, :] * scale - jnp.concatenate([norm, norm], axis=1)
            grown = jnp.exp2(score - jnp.max(score, axis=0, keepdims=True))
            share_scale = own[k : k + 1, :] / jnp.sum(grown, axis=0, keepdims=True)
            store(span, (grown * share_scale).astype(jnp.bfloat16))
            if last:
                cost = cost + share_scale * jnp.sum(grown * score, axis=0, keepdims=True)
        return cost

    def visit(chip):
        find_products(chip, 0)
        find_logits(chip)
        own = find_resp(chip, 0)

        def store(span, value):
            weight_ref[0, span, :] = value

        find_weights(own, 0, store, False)
        weight = weight_ref[0]
        stats_ref[...] += lax.dot_general(
            weight, rows_of(chip), plain, preferred_element_type=f32
        )
        fine_mass_ref[...] += lax.dot_general(weight, ones, plain, preferred_element_type=f32)

    def spread(step, carry):
        left_z, right_z = z - step - 1, z + step + 1
        for span in range(LATE + 2):
            xx = x if span <= LATE else 1 - x
            part = min(span, LATE)

            @pl.when(left_z >= 0)
            def _():
                wait_rows(left_z, xx, s, part)
                send_right(left_z, xx, part, span)
                if part < LATE:
                    to_cross(left_z, part).start()
                to_twin(left_z, xx, part).start()

            @pl.when(right_z < cent_size)
            def _():
                wait_rows(right_z, xx, s, part)
                send_left(right_z, xx, part, span)
                if part < LATE:
                    to_cross(right_z, part).start()
                to_twin(right_z, xx, part).start()

        def place(side):
            zz = z - step + 2 * step * side
            there = jnp.logical_and(zz >= 0, zz < cent_size)
            return zz, jnp.logical_and(there, step + 1 > side)

        def crossed(side, carry):
            zz, there = place(side)

            @pl.when(there)
            def _():
                for span in range(LATE):
                    wait_rows(zz, 1 - x, s, span)
                    to_twin(zz, 1 - x, span).start()

            return carry

        def computed(turn, carry):
            zz, there = place(lax.rem(turn, 2))
            xx = lax.rem(x + turn // 2, 2)

            @pl.when(turn == 2)
            def _():
                lax.fori_loop(0, 2, crossed, 0)

            @pl.when(there)
            def _():
                chip = zz * 2 + xx
                for span in range(len(SPANS)):
                    wait_rows(zz, xx, 1 - s, span)
                for core in range(2):

                    @pl.when(chip * 2 + core != me)
                    def _():
                        copy_lists(chip * 2 + core, lax.rem(me + 1, devices)).wait_recv()

                visit(chip)

            return carry

        lax.fori_loop(0, 4, computed, 0)
        return carry

    lax.fori_loop(0, cent_size, spread, 0)

    own_wide = own_rows[...].astype(f32)
    row_norm = jnp.sum(own_wide * own_wide, axis=1, keepdims=True)
    row_norm = jnp.transpose(jnp.broadcast_to(row_norm, (local_rows, 128)))[0:1, :]

    def new_log_weights():
        total = jnp.sum(mass_ref[...], axis=1, keepdims=True)
        fresh = jnp.log((total + 1.0) / (devices * local_rows + coarse_all))
        log_weights_ref[...] = jnp.broadcast_to(fresh, log_weights_ref.shape)
        mass_ref[...] = jnp.zeros_like(mass_ref)

    for span in spans:
        shrink = 1.0 / (fine_mass_ref[span, :] + 1.0)
        state = stats_ref[span, :] * jnp.concatenate([shrink] * (width // 128), axis=1)
        stats_ref[span, :] = state
        fine_bf_ref[span, :] = state.astype(jnp.bfloat16)
        keep_norm(span, fine_bf_ref[span, :])
    new_log_weights()

    def copy_cost(owner, other):
        return pltpu.make_async_remote_copy(
            src_ref=cost_part_ref.at[other],
            dst_ref=cost_got_ref.at[owner],
            send_sem=cost_send.at[other],
            recv_sem=cost_recv.at[owner],
            device_id=device(other),
            device_id_type=MESH,
        )

    def second(step, carry):
        pair = [lax.rem(z * 2 + x + 2 * step + 1 + i, chips) for i in range(2)]
        for i, chip in enumerate(pair):
            find_products(chip, i)
        for i, chip in enumerate(pair):
            own = find_resp(chip, i)

            def store(span, value):
                weight_ref[chip, span, :] = value

            cost = find_weights(own, i, store, True) * (-2.0 / (scale * width))
            for core in range(2):
                cost_part_ref[chip * 2 + core] = cost[:, core * local_rows : (core + 1) * local_rows]
        for chip in pair:
            for core in range(2):

                @pl.when(chip * 2 + core != me)
                def _():
                    copy_cost(me, chip * 2 + core).start()

        return carry

    lax.fori_loop(0, chips // 2, second, 0)

    weight = jnp.concatenate([weight_ref[chip] for chip in range(chips)], axis=1)
    all_ones = jnp.ones((chips * chunk_rows, 128), jnp.bfloat16)
    shrink = 1.0 / (lax.dot_general(weight, all_ones, plain, preferred_element_type=f32) + 1.0)
    wide_shrink = jnp.concatenate([shrink, shrink], axis=1)
    for start in range(0, width, 256):
        columns = pl.ds(start, 256)
        sums = lax.dot_general(
            weight, rows_all_ref[:, columns], plain, preferred_element_type=f32
        )
        state = (sums + stats_ref[:, columns]) * wide_shrink
        fine_out_ref[:, columns] = state.astype(jnp.bfloat16)
    listed = prob_ref[1]
    resp = listed / jnp.sum(listed, axis=0, keepdims=True)
    resp_sum = jnp.sum(resp.astype(jnp.bfloat16).astype(f32), axis=0, keepdims=True)
    new_log_weights()
    own_weights = log_weights_ref[
        pl.ds(pl.multiple_of(me * clusters_dev, clusters_dev), clusters_dev), :
    ]
    diagonal = lax.broadcasted_iota(jnp.int32, own_weights.shape, 0) == lax.broadcasted_iota(
        jnp.int32, own_weights.shape, 1
    )
    own_weights = jnp.sum(jnp.where(diagonal, own_weights, 0.0), axis=0, keepdims=True)
    weights_out_ref[...] = own_weights[:, :clusters_dev]

    def drain(step, carry):
        other = lax.rem(me + step, devices)
        copy_lists(me, other).wait_send()
        copy_cost(me, other).wait_send()
        return carry

    lax.fori_loop(1, devices, drain, 0)

    def drain_rows(zz, carry):
        for span in range(LATE + 2):
            xx = x if span <= LATE else 1 - x
            part = min(span, LATE)

            @pl.when(jnp.logical_and(z + 1 < cent_size, zz <= z))
            def _():
                to_right(zz, xx, part, span).wait_send()

            @pl.when(jnp.logical_and(z >= 1, zz >= z))
            def _():
                to_left(zz, xx, part, span).wait_send()

        for span in range(LATE):
            to_cross(zz, span).wait_send()
        for span in range(len(SPANS)):
            for xx in range(2):
                to_twin(zz, xx, span).wait_send()
        return carry

    to_cross(z, LATE).wait_send()
    lax.fori_loop(0, cent_size, drain_rows, 0)

    resp_sum = jnp.where(s == 0, resp_sum[:, :local_rows], resp_sum[:, local_rows:])
    total = row_norm * resp_sum * (1.0 / width) + cost_part_ref[me]

    def collect(step, total):
        other = lax.rem(me + step, devices)
        copy_cost(other, other).wait_recv()
        return total + cost_got_ref[other]

    cost_out_ref[...] = lax.fori_loop(1, devices, collect, total)


def write_kernel(fine_ref, cost_ref, weights_ref, fine_out, cost_out, weights_out, sem):
    pairs = ((fine_ref, fine_out), (cost_ref, cost_out), (weights_ref, weights_out))
    copies = [pltpu.make_async_copy(a, b, sem.at[i]) for i, (a, b) in enumerate(pairs)]
    for copy in copies:
        copy.start()
    for copy in copies:
        copy.wait()


def gather_body(cent_size, embeddings, coarse_lists, coarse_table, fine_table):
    local_rows, width = embeddings.shape
    coarse_all = coarse_table.shape[0]
    fine_dev = fine_table.shape[0]
    clusters_dev = fine_dev // FINE_PER
    devices = 4 * cent_size
    chips = 2 * cent_size
    chunk = 2 * local_rows
    f32, bf16 = jnp.float32, jnp.bfloat16
    dma = pltpu.SemaphoreType.DMA
    fine_out, row_cost, own_weights = pl.pallas_call(
        functools.partial(gather_kernel, cent_size),
        out_shape=(
            jax.ShapeDtypeStruct((fine_dev, width), bf16),
            jax.ShapeDtypeStruct((1, local_rows), f32),
            jax.ShapeDtypeStruct((1, clusters_dev), f32),
        ),
        in_specs=[pl.BlockSpec(memory_space=pltpu.HBM)] * 4,
        out_specs=(pl.BlockSpec(memory_space=pltpu.VMEM),) * 3,
        scratch_shapes=[
            pltpu.VMEM((coarse_all, width), bf16),
            pltpu.VMEM((devices * local_rows, width), bf16),
            pltpu.VMEM((devices, TOP, local_rows), jnp.int32),
            pltpu.VMEM((chips, coarse_all, chunk), f32),
            pltpu.VMEM((2, coarse_all, chunk), f32),
            pltpu.VMEM((chips, coarse_all, chunk), f32),
            pltpu.VMEM((coarse_all, 128), f32),
            pltpu.VMEM((fine_dev, width), bf16),
            pltpu.VMEM((fine_dev, 128), f32),
            pltpu.VMEM((2, fine_dev, chunk), f32),
            pltpu.VMEM((chips, fine_dev, chunk), bf16),
            pltpu.VMEM((fine_dev, width), f32),
            pltpu.VMEM((fine_dev, 128), f32),
            pltpu.VMEM((coarse_all, 128), f32),
            pltpu.VMEM((devices, 1, local_rows), f32),
            pltpu.VMEM((devices, 1, local_rows), f32),
            dma((4,)),
            dma((2, cent_size, len(SPANS) + 1)),
            dma((cent_size, len(SPANS))),
            dma((cent_size, 2, len(SPANS))),
            dma((devices, len(SPANS))),
            dma((devices,)),
            dma((devices,)),
            dma((devices,)),
            dma((devices,)),
        ],
        compiler_params=pltpu.CompilerParams(
            collective_id=0, has_side_effects=True, vmem_limit_bytes=60 * 1024 * 1024
        ),
    )(embeddings, coarse_lists.T, coarse_table, fine_table)
    results = (fine_out, row_cost, own_weights)
    fine_out, row_cost, own_weights = pl.pallas_call(
        write_kernel,
        out_shape=tuple(jax.ShapeDtypeStruct(a.shape, a.dtype) for a in results),
        in_specs=[pl.BlockSpec(memory_space=pltpu.VMEM)] * 3,
        out_specs=(pl.BlockSpec(memory_space=pltpu.HBM),) * 3,
        scratch_shapes=[dma((3,))],
    )(*results)
    return fine_out, row_cost.reshape(-1), own_weights.reshape(-1)


def solution(mesh):
    sizes = dict(mesh.shape)

    def body(embeddings, coarse_lists, coarse_table, fine_table):
        devices = sizes["cent"] * sizes["rows"] * sizes["sub"]
        gathered_bytes = 2 * devices * embeddings.size
        fits = gathered_bytes <= GATHER_MAX and embeddings.shape[0] == 128
        fits = fits and fine_table.shape[0] == 8 * FINE_PER
        if sizes["rows"] == 2 and sizes["sub"] == 2 and fits:
            return gather_body(sizes["cent"], embeddings, coarse_lists, coarse_table, fine_table)
        return dispatch_body(embeddings, coarse_lists, coarse_table, fine_table)

    return jax.shard_map(
        body,
        mesh=mesh,
        in_specs=(
            P(("groups", "cent", "rows", "sub"), None),
            P(("groups", "cent", "rows", "sub"), None),
            P(),
            P(("cent", "rows", "sub"), None),
        ),
        out_specs=(
            P(("groups", "cent", "rows", "sub"), None),
            P(("groups", "cent", "rows", "sub")),
            P(("groups", "cent", "rows", "sub")),
        ),
        check_vma=False,
    )
```

```python
import math

import functools

import jax
import jax.numpy as jnp
from jax import lax
from jax.experimental import pallas as pl
from jax.experimental.pallas import tpu as pltpu
from jax.sharding import PartitionSpec as P

FINE_PER = 64
TOP = 8
ITERS = 2


def dispatch_body(embeddings, coarse_lists, coarse_table, fine_table):
    local_rows, model_width = embeddings.shape
    coarse_all = coarse_table.shape[0]
    clusters_dev = fine_table.shape[0] // FINE_PER
    cent_size = lax.axis_size("cent")
    rest_size = lax.axis_size(("rows", "sub"))
    devices = lax.axis_size(("cent", "rows", "sub"))
    rows_all = local_rows * devices
    most_rows = max(2, 2 * local_rows * TOP // coarse_all)
    factor = 1.0 / math.sqrt(model_width)
    slot_total = coarse_all * most_rows
    received = devices * most_rows
    coarse_norm = jnp.einsum(
        "kd,kd->k", coarse_table, coarse_table, preferred_element_type=jnp.float32
    )
    flat_ids = coarse_lists.reshape(-1)
    copies = flat_ids.shape[0]
    order_ids = jnp.argsort(flat_ids, stable=True)
    sorted_ids = flat_ids[order_ids]
    first_seen = jnp.searchsorted(sorted_ids, sorted_ids, side="left")
    sorted_position = jnp.arange(copies, dtype=jnp.int32) - first_seen
    position = jnp.zeros((copies,), jnp.int32).at[order_ids].set(sorted_position)
    slot_index = flat_ids * most_rows + position
    copy_rows = jnp.arange(copies, dtype=jnp.int32) // TOP
    source_row = jnp.full((slot_total,), -1, jnp.int32).at[slot_index].set(copy_rows)
    filled = source_row >= 0
    picked = embeddings[jnp.maximum(source_row, 0)]
    row_buffer = jnp.where(filled[:, None], picked, jnp.zeros_like(picked))
    row_buffer = row_buffer.reshape(cent_size, rest_size, clusters_dev, most_rows * model_width)
    log_weights = jnp.full((coarse_all,), -math.log(coarse_all), jnp.float32)
    fine_state = fine_table.astype(jnp.float32)
    row_cost = jnp.zeros((local_rows,), jnp.float32)
    got_rows = lax.all_to_all(
        lax.all_to_all(row_buffer, "cent", split_axis=0, concat_axis=3, tiled=True),
        ("rows", "sub"),
        split_axis=1,
        concat_axis=3,
        tiled=True,
    )
    for iteration in range(ITERS):
        coarse_dots = jnp.einsum(
            "rd,kd->rk", embeddings, coarse_table, preferred_element_type=jnp.float32
        )
        coarse_prob = jax.nn.softmax((coarse_dots - 0.5 * coarse_norm) * factor + log_weights, -1)
        masses = lax.psum(jnp.sum(coarse_prob, 0), ("cent", "rows", "sub"))
        listed = jnp.take_along_axis(coarse_prob, coarse_lists, 1)
        coarse_resp = (listed / jnp.sum(listed, -1, keepdims=True)).astype(jnp.bfloat16)
        resp_buffer = (
            jnp.zeros((slot_total,), jnp.bfloat16).at[slot_index].set(coarse_resp.reshape(-1))
        )
        resp_buffer = resp_buffer.reshape(cent_size, rest_size, clusters_dev, most_rows)
        got_resp = lax.all_to_all(
            lax.all_to_all(resp_buffer, "cent", split_axis=0, concat_axis=3, tiled=True),
            ("rows", "sub"),
            split_axis=1,
            concat_axis=3,
            tiled=True,
        )
        fine_bf = fine_state.astype(jnp.bfloat16)
        fine_norm = jnp.sum(jnp.square(fine_bf.astype(jnp.float32)), -1).reshape(
            clusters_dev, FINE_PER
        )
        slab_rows = got_rows.reshape(clusters_dev, received, model_width)
        slab_resp = got_resp.reshape(clusters_dev, received).astype(jnp.float32)
        centers = fine_bf.reshape(clusters_dev, FINE_PER, model_width)
        products = jnp.einsum(
            "cjd,csd->cjs", centers, slab_rows, preferred_element_type=jnp.float32
        )
        norm_term = fine_norm[:, :, None]
        shares = jax.nn.softmax((products - 0.5 * norm_term) * factor, 1)
        weight = (slab_resp[:, None, :] * shares).astype(jnp.bfloat16)
        fine_mass = jnp.sum(weight.astype(jnp.float32), 2).reshape(-1)
        stat_sums = jnp.einsum(
            "cjs,csd->cjd", weight, slab_rows, preferred_element_type=jnp.float32
        ).reshape(-1, model_width)
        if iteration == ITERS - 1:
            row_norm = jnp.einsum(
                "csd,csd->cs", slab_rows, slab_rows, preferred_element_type=jnp.float32
            )
            distance = row_norm[:, None, :] - 2.0 * products + norm_term
            slot_cost = slab_resp * jnp.sum(shares * distance, 1) / model_width
            slot_cost = slot_cost.reshape(1, 1, clusters_dev, rest_size, cent_size * most_rows)
            returned = lax.all_to_all(
                lax.all_to_all(slot_cost, "cent", split_axis=4, concat_axis=0, tiled=True),
                ("rows", "sub"),
                split_axis=3,
                concat_axis=1,
                tiled=True,
            )
            row_cost = jnp.sum(returned.reshape(-1)[slot_index].reshape(local_rows, TOP), -1)
        fine_state = (stat_sums + fine_state) / (fine_mass + 1.0)[:, None]
        log_weights = jnp.log((masses + 1.0) / (rows_all + coarse_all))
    device_index = lax.axis_index(("cent", "rows", "sub"))
    own_weights = lax.dynamic_slice_in_dim(log_weights, device_index * clusters_dev, clusters_dev)
    return (fine_state.astype(jnp.bfloat16), row_cost, own_weights)


GATHER_MAX = 8 * 1024 * 1024
PARTS = 4
SPANS = ((0, 64), (64, 48), (112, 16))
LATE = len(SPANS) - 1
MESH = pl.DeviceIdType.MESH


def gather_kernel(
    cent_size,
    emb_ref,
    lists_ref,
    coarse_hbm_ref,
    fine_hbm_ref,
    fine_out_ref,
    cost_out_ref,
    weights_out_ref,
    coarse_ref,
    rows_all_ref,
    lists_all_ref,
    logits_ref,
    prob_ref,
    mask_ref,
    mass_ref,
    fine_bf_ref,
    half_norm_ref,
    products_ref,
    weight_ref,
    stats_ref,
    fine_mass_ref,
    log_weights_ref,
    cost_part_ref,
    cost_got_ref,
    load_sem,
    row_send,
    cross_send,
    twin_send,
    row_recv,
    lists_send,
    lists_recv,
    cost_send,
    cost_recv,
):
    local_rows, width = emb_ref.shape
    coarse_all = coarse_ref.shape[0]
    fine_dev = fine_bf_ref.shape[0]
    clusters_dev = fine_dev // FINE_PER
    devices = 4 * cent_size
    chips = 2 * cent_size
    chunk_rows = 2 * local_rows
    factor = 1.0 / math.sqrt(width)
    group = lax.axis_index("groups")
    z = lax.axis_index("cent")
    x = lax.axis_index("rows")
    s = lax.axis_index("sub")
    me = (z * 2 + x) * 2 + s
    f32 = jnp.float32

    def device(index):
        return (group, index // 4, (index // 2) % 2, index % 2)

    own_rows = rows_all_ref.at[pl.ds(pl.multiple_of(me * local_rows, local_rows), local_rows)]
    load_rows = pltpu.make_async_copy(emb_ref, own_rows, load_sem.at[0])
    load_lists = pltpu.make_async_copy(lists_ref, lists_all_ref.at[me], load_sem.at[1])
    load_coarse = pltpu.make_async_copy(coarse_hbm_ref, coarse_ref, load_sem.at[2])
    load_fine = pltpu.make_async_copy(fine_hbm_ref, fine_bf_ref, load_sem.at[3])
    load_rows.start()
    load_lists.start()
    load_coarse.start()
    load_fine.start()

    barrier = pltpu.get_barrier_semaphore()

    def greet(step, carry):
        other = lax.rem(me + step, devices)
        pl.semaphore_signal(barrier, inc=1, device_id=device(other), device_id_type=MESH)
        return carry

    lax.fori_loop(1, devices, greet, 0)
    pl.semaphore_wait(barrier, devices - 1)

    def copy_rows(zz, xx, ss, span, sem, target):
        owner = (zz * 2 + xx) * 2 + ss
        start, count = SPANS[span]
        place = rows_all_ref.at[pl.ds(pl.multiple_of(owner * local_rows + start, 16), count)]
        return pltpu.make_async_remote_copy(
            src_ref=place,
            dst_ref=place,
            send_sem=sem,
            recv_sem=row_recv.at[owner, span],
            device_id=target,
            device_id_type=MESH,
        )

    def to_right(zz, xx, span, way):
        return copy_rows(zz, xx, s, span, row_send.at[0, zz, way], (group, z + 1, x, s))

    def to_left(zz, xx, span, way):
        return copy_rows(zz, xx, s, span, row_send.at[1, zz, way], (group, z - 1, x, s))

    def to_cross(zz, span):
        return copy_rows(zz, x, s, span, cross_send.at[zz, span], (group, z, 1 - x, s))

    def to_twin(zz, xx, span):
        return copy_rows(zz, xx, s, span, twin_send.at[zz, xx, span], (group, z, x, 1 - s))

    def wait_rows(zz, xx, ss, span):
        copy_rows(zz, xx, ss, span, twin_send.at[0, 0, 0], (group, z, x, 1 - s)).wait_recv()

    def send_right(zz, xx, span, way):
        @pl.when(z + 1 < cent_size)
        def _():
            to_right(zz, xx, span, way).start()

    def send_left(zz, xx, span, way):
        @pl.when(z >= 1)
        def _():
            to_left(zz, xx, span, way).start()

    load_rows.wait()
    to_cross(z, LATE).start()
    for span in range(LATE):
        send_right(z, x, span, span)
        send_left(z, x, span, span)
        to_cross(z, span).start()
    send_right(z, x, LATE, LATE)
    send_left(z, x, LATE, LATE)
    for span in range(len(SPANS)):
        to_twin(z, x, span).start()
    load_lists.wait()

    def copy_lists(owner, other):
        return pltpu.make_async_remote_copy(
            src_ref=lists_all_ref.at[owner],
            dst_ref=lists_all_ref.at[owner],
            send_sem=lists_send.at[other],
            recv_sem=lists_recv.at[owner],
            device_id=device(other),
            device_id_type=MESH,
        )

    def send_lists(step, carry):
        copy_lists(me, lax.rem(me + step, devices)).start()
        return carry

    lax.fori_loop(1, devices, send_lists, 0)

    load_coarse.wait()
    load_fine.wait()
    coarse_wide = coarse_ref[...].astype(f32)
    coarse_half = 0.5 * jnp.sum(coarse_wide * coarse_wide, axis=1, keepdims=True)
    mass_ref[...] = jnp.zeros_like(mass_ref)
    log_weights_ref[...] = jnp.full(log_weights_ref.shape, -math.log(coarse_all), f32)

    scale = factor * math.log2(math.e)

    def keep_norm(span, centers):
        wide = centers.astype(f32)
        norm = (0.5 * scale) * jnp.sum(wide * wide, axis=1, keepdims=True)
        half_norm_ref[span, :] = jnp.broadcast_to(norm, (FINE_PER, 128))

    spans = [pl.ds(k * FINE_PER, FINE_PER) for k in range(clusters_dev)]
    for span in spans:
        keep_norm(span, fine_bf_ref[span, :])
        stats_ref[span, :] = fine_bf_ref[span, :].astype(f32)
    fine_mass_ref[...] = jnp.zeros_like(fine_mass_ref)
    dims = (((1,), (1,)), ((), ()))
    plain = (((1,), (0,)), ((), ()))
    ones = jnp.ones((chunk_rows, 128), jnp.bfloat16)

    def rows_of(chip):
        return rows_all_ref[pl.ds(pl.multiple_of(chip * chunk_rows, chunk_rows), chunk_rows), :]

    def find_products(chip, buffer):
        products_ref[buffer] = lax.dot_general(
            fine_bf_ref[...], rows_of(chip), dims, preferred_element_type=f32
        )

    def find_logits(chip):
        dots = lax.dot_general(coarse_ref[...], rows_of(chip), dims, preferred_element_type=f32)
        logits_ref[chip] = (dots - coarse_half) * factor
        cluster = lax.broadcasted_iota(jnp.int32, (coarse_all, local_rows), 0)
        for core in range(2):
            named = lists_all_ref[chip * 2 + core]
            mask = cluster == named[0:1, :]
            for t in range(1, TOP):
                mask = jnp.logical_or(mask, cluster == named[t : t + 1, :])
            mask_ref[chip, :, core * local_rows : (core + 1) * local_rows] = mask.astype(f32)

    def find_resp(chip, buffer):
        logits = logits_ref[chip] + jnp.concatenate([log_weights_ref[...]] * 2, axis=1)
        raised = jnp.exp(logits - jnp.max(logits, axis=0, keepdims=True))
        prob = raised * (1.0 / jnp.sum(raised, axis=0, keepdims=True))
        mass_ref[...] += prob[:, :128] + prob[:, 128:]
        listed = mask_ref[chip] * prob
        prob_ref[buffer] = listed
        start = pl.multiple_of(me * clusters_dev, clusters_dev)
        own = prob_ref[buffer, pl.ds(start, clusters_dev), :]
        own = own / jnp.sum(listed, axis=0, keepdims=True)
        return own.astype(jnp.bfloat16).astype(f32)

    def find_weights(own, buffer, store, last):
        cost = jnp.zeros((1, chunk_rows), f32)
        for k, span in enumerate(spans):
            norm = half_norm_ref[span, :]
            score = products_ref[buffer, span, :] * scale - jnp.concatenate([norm, norm], axis=1)
            grown = jnp.exp2(score - jnp.max(score, axis=0, keepdims=True))
            share_scale = own[k : k + 1, :] / jnp.sum(grown, axis=0, keepdims=True)
            store(span, (grown * share_scale).astype(jnp.bfloat16))
            if last:
                cost = cost + share_scale * jnp.sum(grown * score, axis=0, keepdims=True)
        return cost

    def visit(chip):
        find_products(chip, 0)
        find_logits(chip)
        own = find_resp(chip, 0)

        def store(span, value):
            weight_ref[0, span, :] = value

        find_weights(own, 0, store, False)
        weight = weight_ref[0]
        stats_ref[...] += lax.dot_general(
            weight, rows_of(chip), plain, preferred_element_type=f32
        )
        fine_mass_ref[...] += lax.dot_general(weight, ones, plain, preferred_element_type=f32)

    def spread(step, carry):
        @pl.when(step == 1)
        def _():
            wait_rows(z, 1 - x, s, LATE)
            send_right(z, 1 - x, LATE, LATE + 1)
            send_left(z, 1 - x, LATE, LATE + 1)
            to_twin(z, 1 - x, LATE).start()

        left_z, right_z = z - step, z + step
        for span in range(LATE + 2):
            xx = x if span <= LATE else 1 - x
            part = min(span, LATE)

            @pl.when(jnp.logical_and(step >= 1, left_z >= 0))
            def _():
                wait_rows(left_z, xx, s, part)
                send_right(left_z, xx, part, span)
                if part < LATE:
                    to_cross(left_z, part).start()
                to_twin(left_z, xx, part).start()

            @pl.when(jnp.logical_and(step >= 1, right_z < cent_size))
            def _():
                wait_rows(right_z, xx, s, part)
                send_left(right_z, xx, part, span)
                if part < LATE:
                    to_cross(right_z, part).start()
                to_twin(right_z, xx, part).start()

        def place(far, side):
            zz = z - far + 2 * far * side
            there = jnp.logical_and(zz >= 0, zz < cent_size)
            return zz, jnp.logical_and(there, far + 1 > side)

        def crossed(side, far):
            zz, there = place(far, side)

            @pl.when(jnp.logical_and(there, far >= 0))
            def _():
                for span in range(LATE):
                    wait_rows(zz, 1 - x, s, span)
                    to_twin(zz, 1 - x, span).start()

            return far

        lax.fori_loop(0, 2, crossed, step - 1)

        def computed(turn, carry):
            other = turn // 2
            zz, there = place(step - other, lax.rem(turn, 2))
            xx = lax.rem(x + other, 2)


            @pl.when(jnp.logical_and(there, step >= other))
            def _():
                chip = zz * 2 + xx
                for span in range(len(SPANS)):
                    wait_rows(zz, xx, 1 - s, span)
                for core in range(2):

                    @pl.when(chip * 2 + core != me)
                    def _():
                        copy_lists(chip * 2 + core, lax.rem(me + 1, devices)).wait_recv()

                visit(chip)

            return carry

        lax.fori_loop(0, 4, computed, 0)
        return carry

    lax.fori_loop(0, cent_size + 1, spread, 0)

    own_wide = own_rows[...].astype(f32)
    row_norm = jnp.sum(own_wide * own_wide, axis=1, keepdims=True)
    row_norm = jnp.transpose(jnp.broadcast_to(row_norm, (local_rows, 128)))[0:1, :]

    def new_log_weights():
        total = jnp.sum(mass_ref[...], axis=1, keepdims=True)
        fresh = jnp.log((total + 1.0) / (devices * local_rows + coarse_all))
        log_weights_ref[...] = jnp.broadcast_to(fresh, log_weights_ref.shape)
        mass_ref[...] = jnp.zeros_like(mass_ref)

    for span in spans:
        shrink = 1.0 / (fine_mass_ref[span, :] + 1.0)
        state = stats_ref[span, :] * jnp.concatenate([shrink] * (width // 128), axis=1)
        stats_ref[span, :] = state
        fine_bf_ref[span, :] = state.astype(jnp.bfloat16)
        keep_norm(span, fine_bf_ref[span, :])
    new_log_weights()

    def copy_cost(owner, other):
        return pltpu.make_async_remote_copy(
            src_ref=cost_part_ref.at[other],
            dst_ref=cost_got_ref.at[owner],
            send_sem=cost_send.at[other],
            recv_sem=cost_recv.at[owner],
            device_id=device(other),
            device_id_type=MESH,
        )

    order = [lax.rem(z * 2 + x + 1 + i, chips) for i in range(chips)]
    find_products(order[0], 0)
    find_products(order[1], 1)
    for i, chip in enumerate(order):
        if i % 2 == 0 and i + 2 < chips:
            find_products(order[i + 2], (i + 2) % 4)
            find_products(order[i + 3], (i + 3) % 4)
        own = find_resp(chip, i % 2)

        def store(span, value):
            weight_ref[chip, span, :] = value

        cost = find_weights(own, i % 4, store, True) * (-2.0 / (scale * width))
        for core in range(2):
            cost_part_ref[chip * 2 + core] = cost[:, core * local_rows : (core + 1) * local_rows]
        if i + 1 < chips:
            copy_cost(me, chip * 2).start()
            copy_cost(me, chip * 2 + 1).start()
        else:
            copy_cost(me, chip * 2 + 1 - s).start()

    weight = jnp.concatenate([weight_ref[chip] for chip in range(chips)], axis=1)
    all_ones = jnp.ones((chips * chunk_rows, 128), jnp.bfloat16)
    shrink = 1.0 / (lax.dot_general(weight, all_ones, plain, preferred_element_type=f32) + 1.0)
    wide_shrink = jnp.concatenate([shrink, shrink], axis=1)
    for start in range(0, width, 256):
        columns = pl.ds(start, 256)
        sums = lax.dot_general(
            weight, rows_all_ref[:, columns], plain, preferred_element_type=f32
        )
        state = (sums + stats_ref[:, columns]) * wide_shrink
        fine_out_ref[:, columns] = state.astype(jnp.bfloat16)
    listed = prob_ref[1]
    resp = listed / jnp.sum(listed, axis=0, keepdims=True)
    resp_sum = jnp.sum(resp.astype(jnp.bfloat16).astype(f32), axis=0, keepdims=True)
    new_log_weights()
    own_weights = log_weights_ref[
        pl.ds(pl.multiple_of(me * clusters_dev, clusters_dev), clusters_dev), :
    ]
    diagonal = lax.broadcasted_iota(jnp.int32, own_weights.shape, 0) == lax.broadcasted_iota(
        jnp.int32, own_weights.shape, 1
    )
    own_weights = jnp.sum(jnp.where(diagonal, own_weights, 0.0), axis=0, keepdims=True)
    weights_out_ref[...] = own_weights[:, :clusters_dev]

    def drain(step, carry):
        other = lax.rem(me + step, devices)
        copy_lists(me, other).wait_send()
        copy_cost(me, other).wait_send()
        return carry

    lax.fori_loop(1, devices, drain, 0)

    def drain_rows(zz, carry):
        for span in range(LATE + 2):
            xx = x if span <= LATE else 1 - x
            part = min(span, LATE)

            @pl.when(jnp.logical_and(z + 1 < cent_size, zz <= z))
            def _():
                to_right(zz, xx, part, span).wait_send()

            @pl.when(jnp.logical_and(z >= 1, zz >= z))
            def _():
                to_left(zz, xx, part, span).wait_send()

        for span in range(LATE):
            to_cross(zz, span).wait_send()
        for span in range(len(SPANS)):
            for xx in range(2):
                to_twin(zz, xx, span).wait_send()
        return carry

    to_cross(z, LATE).wait_send()
    lax.fori_loop(0, cent_size, drain_rows, 0)

    resp_sum = jnp.where(s == 0, resp_sum[:, :local_rows], resp_sum[:, local_rows:])
    total = row_norm * resp_sum * (1.0 / width) + cost_part_ref[me]

    def collect(step, total):
        other = lax.rem(me + step, devices)
        copy_cost(other, other).wait_recv()
        return total + cost_got_ref[other]

    cost_out_ref[...] = lax.fori_loop(1, devices, collect, total)


def write_kernel(fine_ref, cost_ref, weights_ref, fine_out, cost_out, weights_out, *rest):
    fine_held, cost_held, weights_held, sem = rest
    count = fine_ref.shape[0] // PARTS
    hops = [(cost_ref, cost_held, cost_out), (weights_ref, weights_held, weights_out)]
    for part in range(PARTS):
        span = pl.ds(part * count, count)
        hops.append((fine_ref.at[span], fine_held.at[span], fine_out.at[span]))
    inward = [pltpu.make_async_copy(a, b, sem.at[0, i]) for i, (a, b, _) in enumerate(hops)]
    outward = [pltpu.make_async_copy(b, c, sem.at[1, i]) for i, (_, b, c) in enumerate(hops)]
    for copy in inward:
        copy.start()
    for get, put in zip(inward, outward):
        get.wait()
        put.start()
    for copy in outward:
        copy.wait()


def gather_body(cent_size, embeddings, coarse_lists, coarse_table, fine_table):
    local_rows, width = embeddings.shape
    coarse_all = coarse_table.shape[0]
    fine_dev = fine_table.shape[0]
    clusters_dev = fine_dev // FINE_PER
    devices = 4 * cent_size
    chips = 2 * cent_size
    chunk = 2 * local_rows
    f32, bf16 = jnp.float32, jnp.bfloat16
    dma = pltpu.SemaphoreType.DMA
    fine_out, row_cost, own_weights = pl.pallas_call(
        functools.partial(gather_kernel, cent_size),
        out_shape=(
            jax.ShapeDtypeStruct((fine_dev, width), bf16),
            jax.ShapeDtypeStruct((1, local_rows), f32),
            jax.ShapeDtypeStruct((1, clusters_dev), f32),
        ),
        in_specs=[pl.BlockSpec(memory_space=pltpu.HBM)] * 4,
        out_specs=(pl.BlockSpec(memory_space=pltpu.VMEM),) * 3,
        scratch_shapes=[
            pltpu.VMEM((coarse_all, width), bf16),
            pltpu.VMEM((devices * local_rows, width), bf16),
            pltpu.VMEM((devices, TOP, local_rows), jnp.int32),
            pltpu.VMEM((chips, coarse_all, chunk), f32),
            pltpu.VMEM((2, coarse_all, chunk), f32),
            pltpu.VMEM((chips, coarse_all, chunk), f32),
            pltpu.VMEM((coarse_all, 128), f32),
            pltpu.VMEM((fine_dev, width), bf16),
            pltpu.VMEM((fine_dev, 128), f32),
            pltpu.VMEM((4, fine_dev, chunk), f32),
            pltpu.VMEM((chips, fine_dev, chunk), bf16),
            pltpu.VMEM((fine_dev, width), f32),
            pltpu.VMEM((fine_dev, 128), f32),
            pltpu.VMEM((coarse_all, 128), f32),
            pltpu.VMEM((devices, 1, local_rows), f32),
            pltpu.VMEM((devices, 1, local_rows), f32),
            dma((4,)),
            dma((2, cent_size, len(SPANS) + 1)),
            dma((cent_size, len(SPANS))),
            dma((cent_size, 2, len(SPANS))),
            dma((devices, len(SPANS))),
            dma((devices,)),
            dma((devices,)),
            dma((devices,)),
            dma((devices,)),
        ],
        compiler_params=pltpu.CompilerParams(
            collective_id=0, has_side_effects=True, vmem_limit_bytes=60 * 1024 * 1024
        ),
    )(embeddings, coarse_lists.T, coarse_table, fine_table)
    results = (fine_out, row_cost, own_weights)
    fine_out, row_cost, own_weights = pl.pallas_call(
        write_kernel,
        out_shape=tuple(jax.ShapeDtypeStruct(a.shape, a.dtype) for a in results),
        in_specs=[pl.BlockSpec(memory_space=pl.ANY)] * 3,
        out_specs=(pl.BlockSpec(memory_space=pltpu.HBM),) * 3,
        scratch_shapes=[pltpu.VMEM(a.shape, a.dtype) for a in results] + [dma((2, PARTS + 2))],
    )(*results)
    return fine_out, row_cost.reshape(-1), own_weights.reshape(-1)


def solution(mesh):
    sizes = dict(mesh.shape)

    def body(embeddings, coarse_lists, coarse_table, fine_table):
        devices = sizes["cent"] * sizes["rows"] * sizes["sub"]
        gathered_bytes = 2 * devices * embeddings.size
        fits = gathered_bytes <= GATHER_MAX and embeddings.shape[0] == 128
        fits = fits and fine_table.shape[0] == 8 * FINE_PER
        if sizes["rows"] == 2 and sizes["sub"] == 2 and fits:
            return gather_body(sizes["cent"], embeddings, coarse_lists, coarse_table, fine_table)
        return dispatch_body(embeddings, coarse_lists, coarse_table, fine_table)

    return jax.shard_map(
        body,
        mesh=mesh,
        in_specs=(
            P(("groups", "cent", "rows", "sub"), None),
            P(("groups", "cent", "rows", "sub"), None),
            P(),
            P(("cent", "rows", "sub"), None),
        ),
        out_specs=(
            P(("groups", "cent", "rows", "sub"), None),
            P(("groups", "cent", "rows", "sub")),
            P(("groups", "cent", "rows", "sub")),
        ),
        check_vma=False,
    )
```

```python
import math

import functools

import jax
import jax.numpy as jnp
from jax import lax
from jax.experimental import pallas as pl
from jax.experimental.pallas import tpu as pltpu
from jax.sharding import PartitionSpec as P

FINE_PER = 64
TOP = 8
ITERS = 2


def dispatch_body(embeddings, coarse_lists, coarse_table, fine_table):
    local_rows, model_width = embeddings.shape
    coarse_all = coarse_table.shape[0]
    clusters_dev = fine_table.shape[0] // FINE_PER
    cent_size = lax.axis_size("cent")
    rest_size = lax.axis_size(("rows", "sub"))
    devices = lax.axis_size(("cent", "rows", "sub"))
    rows_all = local_rows * devices
    most_rows = max(2, 2 * local_rows * TOP // coarse_all)
    factor = 1.0 / math.sqrt(model_width)
    slot_total = coarse_all * most_rows
    received = devices * most_rows
    coarse_norm = jnp.einsum(
        "kd,kd->k", coarse_table, coarse_table, preferred_element_type=jnp.float32
    )
    flat_ids = coarse_lists.reshape(-1)
    copies = flat_ids.shape[0]
    order_ids = jnp.argsort(flat_ids, stable=True)
    sorted_ids = flat_ids[order_ids]
    first_seen = jnp.searchsorted(sorted_ids, sorted_ids, side="left")
    sorted_position = jnp.arange(copies, dtype=jnp.int32) - first_seen
    position = jnp.zeros((copies,), jnp.int32).at[order_ids].set(sorted_position)
    slot_index = flat_ids * most_rows + position
    copy_rows = jnp.arange(copies, dtype=jnp.int32) // TOP
    source_row = jnp.full((slot_total,), -1, jnp.int32).at[slot_index].set(copy_rows)
    filled = source_row >= 0
    picked = embeddings[jnp.maximum(source_row, 0)]
    row_buffer = jnp.where(filled[:, None], picked, jnp.zeros_like(picked))
    row_buffer = row_buffer.reshape(cent_size, rest_size, clusters_dev, most_rows * model_width)
    log_weights = jnp.full((coarse_all,), -math.log(coarse_all), jnp.float32)
    fine_state = fine_table.astype(jnp.float32)
    row_cost = jnp.zeros((local_rows,), jnp.float32)
    got_rows = lax.all_to_all(
        lax.all_to_all(row_buffer, "cent", split_axis=0, concat_axis=3, tiled=True),
        ("rows", "sub"),
        split_axis=1,
        concat_axis=3,
        tiled=True,
    )
    for iteration in range(ITERS):
        coarse_dots = jnp.einsum(
            "rd,kd->rk", embeddings, coarse_table, preferred_element_type=jnp.float32
        )
        coarse_prob = jax.nn.softmax((coarse_dots - 0.5 * coarse_norm) * factor + log_weights, -1)
        masses = lax.psum(jnp.sum(coarse_prob, 0), ("cent", "rows", "sub"))
        listed = jnp.take_along_axis(coarse_prob, coarse_lists, 1)
        coarse_resp = (listed / jnp.sum(listed, -1, keepdims=True)).astype(jnp.bfloat16)
        resp_buffer = (
            jnp.zeros((slot_total,), jnp.bfloat16).at[slot_index].set(coarse_resp.reshape(-1))
        )
        resp_buffer = resp_buffer.reshape(cent_size, rest_size, clusters_dev, most_rows)
        got_resp = lax.all_to_all(
            lax.all_to_all(resp_buffer, "cent", split_axis=0, concat_axis=3, tiled=True),
            ("rows", "sub"),
            split_axis=1,
            concat_axis=3,
            tiled=True,
        )
        fine_bf = fine_state.astype(jnp.bfloat16)
        fine_norm = jnp.sum(jnp.square(fine_bf.astype(jnp.float32)), -1).reshape(
            clusters_dev, FINE_PER
        )
        slab_rows = got_rows.reshape(clusters_dev, received, model_width)
        slab_resp = got_resp.reshape(clusters_dev, received).astype(jnp.float32)
        centers = fine_bf.reshape(clusters_dev, FINE_PER, model_width)
        products = jnp.einsum(
            "cjd,csd->cjs", centers, slab_rows, preferred_element_type=jnp.float32
        )
        norm_term = fine_norm[:, :, None]
        shares = jax.nn.softmax((products - 0.5 * norm_term) * factor, 1)
        weight = (slab_resp[:, None, :] * shares).astype(jnp.bfloat16)
        fine_mass = jnp.sum(weight.astype(jnp.float32), 2).reshape(-1)
        stat_sums = jnp.einsum(
            "cjs,csd->cjd", weight, slab_rows, preferred_element_type=jnp.float32
        ).reshape(-1, model_width)
        if iteration == ITERS - 1:
            row_norm = jnp.einsum(
                "csd,csd->cs", slab_rows, slab_rows, preferred_element_type=jnp.float32
            )
            distance = row_norm[:, None, :] - 2.0 * products + norm_term
            slot_cost = slab_resp * jnp.sum(shares * distance, 1) / model_width
            slot_cost = slot_cost.reshape(1, 1, clusters_dev, rest_size, cent_size * most_rows)
            returned = lax.all_to_all(
                lax.all_to_all(slot_cost, "cent", split_axis=4, concat_axis=0, tiled=True),
                ("rows", "sub"),
                split_axis=3,
                concat_axis=1,
                tiled=True,
            )
            row_cost = jnp.sum(returned.reshape(-1)[slot_index].reshape(local_rows, TOP), -1)
        fine_state = (stat_sums + fine_state) / (fine_mass + 1.0)[:, None]
        log_weights = jnp.log((masses + 1.0) / (rows_all + coarse_all))
    device_index = lax.axis_index(("cent", "rows", "sub"))
    own_weights = lax.dynamic_slice_in_dim(log_weights, device_index * clusters_dev, clusters_dev)
    return (fine_state.astype(jnp.bfloat16), row_cost, own_weights)


GATHER_MAX = 8 * 1024 * 1024
PARTS = 4
SPANS = ((0, 64), (64, 48), (112, 16))
LATE = len(SPANS) - 1
NAMES = LATE + 1
MESH = pl.DeviceIdType.MESH


def gather_kernel(
    cent_size,
    emb_ref,
    lists_ref,
    coarse_hbm_ref,
    fine_hbm_ref,
    fine_out_ref,
    cost_out_ref,
    weights_out_ref,
    coarse_ref,
    rows_all_ref,
    lists_all_ref,
    logits_ref,
    prob_ref,
    mask_ref,
    mass_ref,
    fine_bf_ref,
    half_norm_ref,
    products_ref,
    weight_ref,
    stats_ref,
    fine_mass_ref,
    log_weights_ref,
    cost_part_ref,
    cost_got_ref,
    load_sem,
    row_send,
    cross_send,
    twin_send,
    row_recv,
    cost_send,
    cost_recv,
):
    local_rows, width = emb_ref.shape
    coarse_all = coarse_ref.shape[0]
    fine_dev = fine_bf_ref.shape[0]
    clusters_dev = fine_dev // FINE_PER
    devices = 4 * cent_size
    chips = 2 * cent_size
    chunk_rows = 2 * local_rows
    factor = 1.0 / math.sqrt(width)
    group = lax.axis_index("groups")
    z = lax.axis_index("cent")
    x = lax.axis_index("rows")
    s = lax.axis_index("sub")
    me = (z * 2 + x) * 2 + s
    f32 = jnp.float32

    def device(index):
        return (group, index // 4, (index // 2) % 2, index % 2)

    own_rows = rows_all_ref.at[pl.ds(pl.multiple_of(me * local_rows, local_rows), local_rows)]
    load_rows = pltpu.make_async_copy(emb_ref, own_rows, load_sem.at[0])
    load_lists = pltpu.make_async_copy(lists_ref, lists_all_ref.at[me], load_sem.at[1])
    load_coarse = pltpu.make_async_copy(coarse_hbm_ref, coarse_ref, load_sem.at[2])
    load_fine = pltpu.make_async_copy(fine_hbm_ref, fine_bf_ref, load_sem.at[3])
    load_rows.start()
    load_lists.start()
    load_coarse.start()
    load_fine.start()

    barrier = pltpu.get_barrier_semaphore()

    def greet(step, carry):
        other = lax.rem(me + step, devices)
        pl.semaphore_signal(barrier, inc=1, device_id=device(other), device_id_type=MESH)
        return carry

    lax.fori_loop(1, devices, greet, 0)
    pl.semaphore_wait(barrier, devices - 1)

    def copy_rows(zz, xx, ss, span, sem, target):
        owner = (zz * 2 + xx) * 2 + ss
        if span == NAMES:
            place = lists_all_ref.at[owner]
        else:
            start, count = SPANS[span]
            place = rows_all_ref.at[pl.ds(pl.multiple_of(owner * local_rows + start, 16), count)]
        return pltpu.make_async_remote_copy(
            src_ref=place,
            dst_ref=place,
            send_sem=sem,
            recv_sem=row_recv.at[owner, span],
            device_id=target,
            device_id_type=MESH,
        )

    def to_right(zz, xx, span, way):
        return copy_rows(zz, xx, s, span, row_send.at[0, zz, way], (group, z + 1, x, s))

    def to_left(zz, xx, span, way):
        return copy_rows(zz, xx, s, span, row_send.at[1, zz, way], (group, z - 1, x, s))

    def to_cross(zz, span):
        return copy_rows(zz, x, s, span, cross_send.at[zz, span], (group, z, 1 - x, s))

    def to_twin(zz, xx, span):
        return copy_rows(zz, xx, s, span, twin_send.at[zz, xx, span], (group, z, x, 1 - s))

    def wait_rows(zz, xx, ss, span):
        copy_rows(zz, xx, ss, span, twin_send.at[0, 0, 0], (group, z, x, 1 - s)).wait_recv()

    def send_right(zz, xx, span, way):
        @pl.when(z + 1 < cent_size)
        def _():
            to_right(zz, xx, span, way).start()

    def send_left(zz, xx, span, way):
        @pl.when(z >= 1)
        def _():
            to_left(zz, xx, span, way).start()

    ways = [(span, x, span) for span in range(NAMES + 1)]
    ways += [(NAMES + 1, 1 - x, LATE), (NAMES + 2, 1 - x, NAMES)]
    load_rows.wait()
    to_cross(z, LATE).start()
    load_lists.wait()
    to_cross(z, NAMES).start()
    for span in range(LATE):
        send_right(z, x, span, span)
        send_left(z, x, span, span)
        to_cross(z, span).start()
    for span in (LATE, NAMES):
        send_right(z, x, span, span)
        send_left(z, x, span, span)
    for span in range(NAMES + 1):
        to_twin(z, x, span).start()

    load_coarse.wait()
    load_fine.wait()
    coarse_wide = coarse_ref[...].astype(f32)
    coarse_half = 0.5 * jnp.sum(coarse_wide * coarse_wide, axis=1, keepdims=True)
    mass_ref[...] = jnp.zeros_like(mass_ref)
    log_weights_ref[...] = jnp.full(log_weights_ref.shape, -math.log(coarse_all), f32)

    scale = factor * math.log2(math.e)

    def keep_norm(span, centers):
        wide = centers.astype(f32)
        norm = (0.5 * scale) * jnp.sum(wide * wide, axis=1, keepdims=True)
        half_norm_ref[span, :] = jnp.broadcast_to(norm, (FINE_PER, 128))

    spans = [pl.ds(k * FINE_PER, FINE_PER) for k in range(clusters_dev)]
    for span in spans:
        keep_norm(span, fine_bf_ref[span, :])
        stats_ref[span, :] = fine_bf_ref[span, :].astype(f32)
    fine_mass_ref[...] = jnp.zeros_like(fine_mass_ref)
    dims = (((1,), (1,)), ((), ()))
    plain = (((1,), (0,)), ((), ()))
    ones = jnp.ones((chunk_rows, 128), jnp.bfloat16)

    def rows_of(chip):
        return rows_all_ref[pl.ds(pl.multiple_of(chip * chunk_rows, chunk_rows), chunk_rows), :]

    def find_products(chip, buffer):
        products_ref[buffer] = lax.dot_general(
            fine_bf_ref[...], rows_of(chip), dims, preferred_element_type=f32
        )

    def find_logits(chip):
        dots = lax.dot_general(coarse_ref[...], rows_of(chip), dims, preferred_element_type=f32)
        logits_ref[chip] = (dots - coarse_half) * factor
        cluster = lax.broadcasted_iota(jnp.int32, (coarse_all, local_rows), 0)
        for core in range(2):
            named = lists_all_ref[chip * 2 + core]
            mask = cluster == named[0:1, :]
            for t in range(1, TOP):
                mask = jnp.logical_or(mask, cluster == named[t : t + 1, :])
            mask_ref[chip, :, core * local_rows : (core + 1) * local_rows] = mask.astype(f32)

    def find_resp(chip, buffer):
        logits = logits_ref[chip] + jnp.concatenate([log_weights_ref[...]] * 2, axis=1)
        raised = jnp.exp(logits - jnp.max(logits, axis=0, keepdims=True))
        prob = raised * (1.0 / jnp.sum(raised, axis=0, keepdims=True))
        mass_ref[...] += prob[:, :128] + prob[:, 128:]
        listed = mask_ref[chip] * prob
        prob_ref[buffer] = listed
        start = pl.multiple_of(me * clusters_dev, clusters_dev)
        own = prob_ref[buffer, pl.ds(start, clusters_dev), :]
        own = own / jnp.sum(listed, axis=0, keepdims=True)
        return own.astype(jnp.bfloat16).astype(f32)

    def find_weights(own, buffer, store, last):
        cost = jnp.zeros((1, chunk_rows), f32)
        for k, span in enumerate(spans):
            norm = half_norm_ref[span, :]
            score = products_ref[buffer, span, :] * scale - jnp.concatenate([norm, norm], axis=1)
            grown = jnp.exp2(score - jnp.max(score, axis=0, keepdims=True))
            share_scale = own[k : k + 1, :] / jnp.sum(grown, axis=0, keepdims=True)
            store(span, (grown * share_scale).astype(jnp.bfloat16))
            if last:
                cost = cost + share_scale * jnp.sum(grown * score, axis=0, keepdims=True)
        return cost

    def visit(chip):
        find_products(chip, 0)
        find_logits(chip)
        own = find_resp(chip, 0)

        def store(span, value):
            weight_ref[0, span, :] = value

        find_weights(own, 0, store, False)
        weight = weight_ref[0]
        stats_ref[...] += lax.dot_general(
            weight, rows_of(chip), plain, preferred_element_type=f32
        )
        fine_mass_ref[...] += lax.dot_general(weight, ones, plain, preferred_element_type=f32)

    def spread(step, carry):
        @pl.when(step == 1)
        def _():
            for way, xx, part in ways[NAMES + 1 :]:
                wait_rows(z, xx, s, part)
                send_right(z, xx, part, way)
                send_left(z, xx, part, way)
                to_twin(z, xx, part).start()

        left_z, right_z = z - step, z + step
        for way, xx, part in ways:

            @pl.when(jnp.logical_and(step >= 1, left_z >= 0))
            def _():
                wait_rows(left_z, xx, s, part)
                send_right(left_z, xx, part, way)
                if part < LATE:
                    to_cross(left_z, part).start()
                to_twin(left_z, xx, part).start()

            @pl.when(jnp.logical_and(step >= 1, right_z < cent_size))
            def _():
                wait_rows(right_z, xx, s, part)
                send_left(right_z, xx, part, way)
                if part < LATE:
                    to_cross(right_z, part).start()
                to_twin(right_z, xx, part).start()

        def place(far, side):
            zz = z - far + 2 * far * side
            there = jnp.logical_and(zz >= 0, zz < cent_size)
            return zz, jnp.logical_and(there, far + 1 > side)

        def crossed(side, far):
            zz, there = place(far, side)

            @pl.when(jnp.logical_and(there, far >= 0))
            def _():
                for span in range(LATE):
                    wait_rows(zz, 1 - x, s, span)
                    to_twin(zz, 1 - x, span).start()

            return far

        lax.fori_loop(0, 2, crossed, step - 1)

        def computed(turn, carry):
            other = turn // 2
            zz, there = place(step - other, lax.rem(turn, 2))
            xx = lax.rem(x + other, 2)


            @pl.when(jnp.logical_and(there, step >= other))
            def _():
                chip = zz * 2 + xx
                for span in range(NAMES + 1):
                    wait_rows(zz, xx, 1 - s, span)
                visit(chip)

            return carry

        lax.fori_loop(0, 4, computed, 0)
        return carry

    lax.fori_loop(0, cent_size + 1, spread, 0)

    own_wide = own_rows[...].astype(f32)
    row_norm = jnp.sum(own_wide * own_wide, axis=1, keepdims=True)
    row_norm = jnp.transpose(jnp.broadcast_to(row_norm, (local_rows, 128)))[0:1, :]

    def new_log_weights():
        total = jnp.sum(mass_ref[...], axis=1, keepdims=True)
        fresh = jnp.log((total + 1.0) / (devices * local_rows + coarse_all))
        log_weights_ref[...] = jnp.broadcast_to(fresh, log_weights_ref.shape)
        mass_ref[...] = jnp.zeros_like(mass_ref)

    for span in spans:
        shrink = 1.0 / (fine_mass_ref[span, :] + 1.0)
        state = stats_ref[span, :] * jnp.concatenate([shrink] * (width // 128), axis=1)
        stats_ref[span, :] = state
        fine_bf_ref[span, :] = state.astype(jnp.bfloat16)
        keep_norm(span, fine_bf_ref[span, :])
    new_log_weights()

    def copy_cost(owner, other):
        return pltpu.make_async_remote_copy(
            src_ref=cost_part_ref.at[other],
            dst_ref=cost_got_ref.at[owner],
            send_sem=cost_send.at[other],
            recv_sem=cost_recv.at[owner],
            device_id=device(other),
            device_id_type=MESH,
        )

    order = [lax.rem(z * 2 + x + 1 + i, chips) for i in range(chips)]
    find_products(order[0], 0)
    find_products(order[1], 1)
    for i, chip in enumerate(order):
        if i % 2 == 0 and i + 2 < chips:
            find_products(order[i + 2], (i + 2) % 4)
            find_products(order[i + 3], (i + 3) % 4)
        own = find_resp(chip, i % 2)

        def store(span, value):
            weight_ref[chip, span, :] = value

        cost = find_weights(own, i % 4, store, True) * (-2.0 / (scale * width))
        for core in range(2):
            cost_part_ref[chip * 2 + core] = cost[:, core * local_rows : (core + 1) * local_rows]
        if i + 1 < chips:
            copy_cost(me, chip * 2).start()
            copy_cost(me, chip * 2 + 1).start()
        else:
            copy_cost(me, chip * 2 + 1 - s).start()

    weight = jnp.concatenate([weight_ref[chip] for chip in range(chips)], axis=1)
    all_ones = jnp.ones((chips * chunk_rows, 128), jnp.bfloat16)
    shrink = 1.0 / (lax.dot_general(weight, all_ones, plain, preferred_element_type=f32) + 1.0)
    wide_shrink = jnp.concatenate([shrink, shrink], axis=1)
    for start in range(0, width, 256):
        columns = pl.ds(start, 256)
        sums = lax.dot_general(
            weight, rows_all_ref[:, columns], plain, preferred_element_type=f32
        )
        state = (sums + stats_ref[:, columns]) * wide_shrink
        fine_out_ref[:, columns] = state.astype(jnp.bfloat16)
    listed = prob_ref[1]
    resp = listed / jnp.sum(listed, axis=0, keepdims=True)
    resp_sum = jnp.sum(resp.astype(jnp.bfloat16).astype(f32), axis=0, keepdims=True)
    new_log_weights()
    own_weights = log_weights_ref[
        pl.ds(pl.multiple_of(me * clusters_dev, clusters_dev), clusters_dev), :
    ]
    diagonal = lax.broadcasted_iota(jnp.int32, own_weights.shape, 0) == lax.broadcasted_iota(
        jnp.int32, own_weights.shape, 1
    )
    own_weights = jnp.sum(jnp.where(diagonal, own_weights, 0.0), axis=0, keepdims=True)
    weights_out_ref[...] = own_weights[:, :clusters_dev]

    def drain(step, carry):
        other = lax.rem(me + step, devices)
        copy_cost(me, other).wait_send()
        return carry

    lax.fori_loop(1, devices, drain, 0)

    def drain_rows(zz, carry):
        for way, xx, part in ways:

            @pl.when(jnp.logical_and(z + 1 < cent_size, zz <= z))
            def _():
                to_right(zz, xx, part, way).wait_send()

            @pl.when(jnp.logical_and(z >= 1, zz >= z))
            def _():
                to_left(zz, xx, part, way).wait_send()

        for span in range(LATE):
            to_cross(zz, span).wait_send()
        for span in range(NAMES + 1):
            for xx in range(2):
                to_twin(zz, xx, span).wait_send()
        return carry

    to_cross(z, LATE).wait_send()
    to_cross(z, NAMES).wait_send()
    lax.fori_loop(0, cent_size, drain_rows, 0)

    resp_sum = jnp.where(s == 0, resp_sum[:, :local_rows], resp_sum[:, local_rows:])
    total = row_norm * resp_sum * (1.0 / width) + cost_part_ref[me]

    def collect(step, total):
        other = lax.rem(me + step, devices)
        copy_cost(other, other).wait_recv()
        return total + cost_got_ref[other]

    cost_out_ref[...] = lax.fori_loop(1, devices, collect, total)


def write_kernel(fine_ref, cost_ref, weights_ref, fine_out, cost_out, weights_out, *rest):
    fine_held, cost_held, weights_held, sem = rest
    count = fine_ref.shape[0] // PARTS
    hops = [(cost_ref, cost_held, cost_out), (weights_ref, weights_held, weights_out)]
    for part in range(PARTS):
        span = pl.ds(part * count, count)
        hops.append((fine_ref.at[span], fine_held.at[span], fine_out.at[span]))
    inward = [pltpu.make_async_copy(a, b, sem.at[0, i]) for i, (a, b, _) in enumerate(hops)]
    outward = [pltpu.make_async_copy(b, c, sem.at[1, i]) for i, (_, b, c) in enumerate(hops)]
    for copy in inward:
        copy.start()
    for get, put in zip(inward, outward):
        get.wait()
        put.start()
    for copy in outward:
        copy.wait()


def gather_body(cent_size, embeddings, coarse_lists, coarse_table, fine_table):
    local_rows, width = embeddings.shape
    coarse_all = coarse_table.shape[0]
    fine_dev = fine_table.shape[0]
    clusters_dev = fine_dev // FINE_PER
    devices = 4 * cent_size
    chips = 2 * cent_size
    chunk = 2 * local_rows
    f32, bf16 = jnp.float32, jnp.bfloat16
    dma = pltpu.SemaphoreType.DMA
    fine_out, row_cost, own_weights = pl.pallas_call(
        functools.partial(gather_kernel, cent_size),
        out_shape=(
            jax.ShapeDtypeStruct((fine_dev, width), bf16),
            jax.ShapeDtypeStruct((1, local_rows), f32),
            jax.ShapeDtypeStruct((1, clusters_dev), f32),
        ),
        in_specs=[pl.BlockSpec(memory_space=pltpu.HBM)] * 4,
        out_specs=(pl.BlockSpec(memory_space=pltpu.VMEM),) * 3,
        scratch_shapes=[
            pltpu.VMEM((coarse_all, width), bf16),
            pltpu.VMEM((devices * local_rows, width), bf16),
            pltpu.VMEM((devices, TOP, local_rows), jnp.int32),
            pltpu.VMEM((chips, coarse_all, chunk), f32),
            pltpu.VMEM((2, coarse_all, chunk), f32),
            pltpu.VMEM((chips, coarse_all, chunk), f32),
            pltpu.VMEM((coarse_all, 128), f32),
            pltpu.VMEM((fine_dev, width), bf16),
            pltpu.VMEM((fine_dev, 128), f32),
            pltpu.VMEM((4, fine_dev, chunk), f32),
            pltpu.VMEM((chips, fine_dev, chunk), bf16),
            pltpu.VMEM((fine_dev, width), f32),
            pltpu.VMEM((fine_dev, 128), f32),
            pltpu.VMEM((coarse_all, 128), f32),
            pltpu.VMEM((devices, 1, local_rows), f32),
            pltpu.VMEM((devices, 1, local_rows), f32),
            dma((4,)),
            dma((2, cent_size, NAMES + 3)),
            dma((cent_size, NAMES + 1)),
            dma((cent_size, 2, NAMES + 1)),
            dma((devices, NAMES + 1)),
            dma((devices,)),
            dma((devices,)),
        ],
        compiler_params=pltpu.CompilerParams(
            collective_id=0, has_side_effects=True, vmem_limit_bytes=60 * 1024 * 1024
        ),
    )(embeddings, coarse_lists.T, coarse_table, fine_table)
    results = (fine_out, row_cost, own_weights)
    fine_out, row_cost, own_weights = pl.pallas_call(
        write_kernel,
        out_shape=tuple(jax.ShapeDtypeStruct(a.shape, a.dtype) for a in results),
        in_specs=[pl.BlockSpec(memory_space=pl.ANY)] * 3,
        out_specs=(pl.BlockSpec(memory_space=pltpu.HBM),) * 3,
        scratch_shapes=[pltpu.VMEM(a.shape, a.dtype) for a in results] + [dma((2, PARTS + 2))],
    )(*results)
    return fine_out, row_cost.reshape(-1), own_weights.reshape(-1)


def solution(mesh):
    sizes = dict(mesh.shape)

    def body(embeddings, coarse_lists, coarse_table, fine_table):
        devices = sizes["cent"] * sizes["rows"] * sizes["sub"]
        gathered_bytes = 2 * devices * embeddings.size
        fits = gathered_bytes <= GATHER_MAX and embeddings.shape[0] == 128
        fits = fits and fine_table.shape[0] == 8 * FINE_PER
        if sizes["rows"] == 2 and sizes["sub"] == 2 and fits:
            return gather_body(sizes["cent"], embeddings, coarse_lists, coarse_table, fine_table)
        return dispatch_body(embeddings, coarse_lists, coarse_table, fine_table)

    return jax.shard_map(
        body,
        mesh=mesh,
        in_specs=(
            P(("groups", "cent", "rows", "sub"), None),
            P(("groups", "cent", "rows", "sub"), None),
            P(),
            P(("cent", "rows", "sub"), None),
        ),
        out_specs=(
            P(("groups", "cent", "rows", "sub"), None),
            P(("groups", "cent", "rows", "sub")),
            P(("groups", "cent", "rows", "sub")),
        ),
        check_vma=False,
    )
```
